32 devices in a mesh: level: 4 (over y, x), req: 8 (over z, core).
Axes of the slice: x: 2, y: 2, z: 4, core: 2. Of those that a mesh axis runs over, the one named last changes fastest.
Arguments:
- queries: bfloat16 [256, 64, 896], P('level', 'req'), may hold values from -120 to 120
- out_grad: bfloat16 [256, 64, 896], P('level', 'req'), may hold values from -5 to 5
- resp_key: bfloat16 [256, 64, 128], P('level', 'req'), may hold values from -4 to 4
- resp_value: bfloat16 [256, 64, 128], P('level', 'req'), may hold values from -4 to 4
- sys_key: bfloat16 [128, 128], P('level'), may hold values from -4 to 4
- sys_value: bfloat16 [128, 128], P('level'), may hold values from -4 to 4
- ctx_key: bfloat16 [16, 128, 128], P('req', 'level'), may hold values from -4 to 4
- ctx_value: bfloat16 [16, 128, 128], P('req', 'level'), may hold values from -4 to 4
- parent: int32 [64], P('req'), may hold values from 0 to 15, as said below
- resp_len: int32 [64], P('req'), may hold values from 64 to 256
- ctx_len: int32 [16], P('req'), may hold values from 32 to 128
Outputs:
- d_queries: float32 [256, 64, 896], P('level', 'req')
- d_sys_key: float32 [128, 128], P(('level', 'req'))
- d_sys_value: float32 [128, 128], P(('level', 'req'))
- d_ctx_key: float32 [16, 128, 128], P('req', 'level')
- d_ctx_value: float32 [16, 128, 128], P('req', 'level')
- d_resp_key: float32 [256, 64, 128], P('level', 'req')
- d_resp_value: float32 [256, 64, 128], P('level', 'req')
The draws below stay inside these ranges and needn't reach their ends.
Inputs may be any that keep to these rules, and one draw needn't show every extreme that they name: Response i's parent is one of the contexts (i // 8) * 2 to (i // 8 + 1) * 2 - 1.
All inputs are finite; a program needn't handle non-finite values.
Results may differ from the reference program's by a relative error of at most 0.0049.
Values may be sent and summed in bfloat16 or wider, within the bound.
A program may use at most 64 MiB of HBM per device.

```python
import jax
import jax.numpy as jnp
from jax import lax

HEADS = 7
HEAD_DIM = 128
CH = 256
CTX_PER = 2
RESP_DEV = 8
RESP = 64
SYS = 128
CTX = 128
CTXS = 16


def base_keys(key):
    return jax.random.truncated_normal(jax.random.fold_in(key, 500), -4.0, 4.0, (SYS, HEAD_DIM), jnp.float32)


def draw_sys_key(key, part):
    shared = base_keys(key)
    return shared.astype(jnp.bfloat16)


def draw_queries(key, part):
    key = jax.random.fold_in(key, 2)
    return jax.random.truncated_normal(key, -4.0, 4.0, (CH, RESP, HEADS * HEAD_DIM), jnp.float32).astype(jnp.bfloat16)


def draw_parent(key, part):
    key = jax.random.fold_in(key, 3)
    owners = jnp.arange(RESP, dtype=jnp.int32) // RESP_DEV
    picks = jax.random.randint(key, (RESP,), 0, CTX_PER, jnp.int32)
    chosen = owners * CTX_PER + picks
    chosen = chosen.at[0].set(0)
    chosen = chosen.at[RESP - 1].set(CTXS - 1)
    return chosen


def draw_resp_len(key, part):
    key = jax.random.fold_in(key, 4)
    lengths = jax.random.randint(key, (RESP,), CH // 4, CH + 1, jnp.int32)
    lengths = lengths.at[0].set(CH)
    lengths = lengths.at[1].set(CH // 4)
    return lengths


def draw_ctx_len(key, part):
    key = jax.random.fold_in(key, 5)
    lengths = jax.random.randint(key, (CTXS,), CTX // 4, CTX + 1, jnp.int32)
    lengths = lengths.at[0].set(CTX)
    lengths = lengths.at[1].set(CTX // 4)
    return lengths


def levels(own_key, shape, pieces, least, top_value):
    gain = 1.0
    for axis_at, shards_of in pieces:
        steps = jax.random.uniform(jax.random.fold_in(jax.random.fold_in(own_key, 6), axis_at), (shards_of,), jnp.float32, least / len(pieces), top_value / len(pieces))
        gain = gain * jnp.repeat(jnp.exp(steps), shape[axis_at] // shards_of).reshape((-1,) + (1,) * (len(shape) - 1 - axis_at))
    return gain


def gaussian(stream_key, extent, width, bound, pieces=(), kind=jnp.bfloat16):
    drawn = width * jax.random.normal(stream_key, extent, jnp.float32)
    if pieces:
        drawn = drawn * levels(stream_key, extent, pieces, -0.22, 0.18)
    return jnp.clip(drawn, -bound, bound).astype(kind)


def setup_inputs(seed: int = 0) -> dict:
    key_of = jax.random.split(jax.random.key(seed), 12)
    queries = draw_queries(jax.random.fold_in(key_of[11], 71), 0)
    out_grad = gaussian(key_of[1], (CH, RESP, HEADS * HEAD_DIM), 1.0, 5.0, ((0, 4), (1, 8)))
    resp_key = gaussian(key_of[2], (CH, RESP, HEAD_DIM), 1.0, 4.0, ((0, 4), (1, 8)))
    resp_value = gaussian(key_of[3], (CH, RESP, HEAD_DIM), 1.0, 4.0, ((0, 4), (1, 8)))
    sys_key = draw_sys_key(jax.random.fold_in(key_of[11], 71), 0)
    sys_value = gaussian(key_of[5], (SYS, HEAD_DIM), 1.0, 4.0, ((0, 4),))
    ctx_key = gaussian(key_of[6], (CTXS, CTX, HEAD_DIM), 1.0, 4.0, ((0, 8), (1, 4)))
    ctx_value = gaussian(key_of[7], (CTXS, CTX, HEAD_DIM), 1.0, 4.0, ((0, 8), (1, 4)))
    parent = draw_parent(jax.random.fold_in(key_of[11], 71), 0)
    resp_len = draw_resp_len(jax.random.fold_in(key_of[11], 71), 0)
    ctx_len = draw_ctx_len(jax.random.fold_in(key_of[11], 71), 0)
    return dict(queries=queries, out_grad=out_grad, resp_key=resp_key, resp_value=resp_value, sys_key=sys_key, sys_value=sys_value, ctx_key=ctx_key, ctx_value=ctx_value, parent=parent, resp_len=resp_len, ctx_len=ctx_len)


NEGATIVE = -1.0e30


def one_response(queries_one, grads_one, key_rows, value_rows, allowed):
    scaling = HEAD_DIM ** -0.5
    key_float = key_rows.astype(jnp.float32)
    value_float = value_rows.astype(jnp.float32)
    query_float = queries_one.astype(jnp.float32)
    grad_float = grads_one.astype(jnp.float32)
    scores = jnp.einsum("kd,thd->kht", key_float, query_float) * scaling
    maxima = jnp.max(jnp.where(allowed, scores, NEGATIVE), axis=0)
    totals = jnp.sum(jnp.where(allowed, jnp.exp(scores - maxima[None]), 0.0), axis=0)
    logsum = maxima + jnp.log(totals)
    chances = jnp.where(allowed, jnp.exp(scores - logsum[None]), 0.0)
    attn_out = jnp.einsum("kht,kd->thd", chances, value_float, precision=lax.Precision.HIGHEST)
    deltas = jnp.sum(grad_float * attn_out, axis=2)
    products = jnp.einsum("kd,thd->kht", value_float, grad_float)
    slopes = lax.optimization_barrier((chances * (products - deltas.T[None])).astype(jnp.bfloat16))
    chances_low = lax.optimization_barrier(chances.astype(jnp.bfloat16))
    slope_float = slopes.astype(jnp.float32)
    query_grad = scaling * jnp.einsum("kht,kd->thd", slope_float, key_float)
    key_grad = scaling * jnp.einsum("kht,thd->kd", slope_float, query_float)
    value_grad = jnp.einsum("kht,thd->kd", chances_low.astype(jnp.float32), grad_float)
    return query_grad, key_grad, value_grad


def reference(queries, out_grad, resp_key, resp_value, sys_key, sys_value, ctx_key, ctx_value, parent, resp_len, ctx_len):
    rows_all = jnp.arange(CH, dtype=jnp.int32)
    ctx_places = jnp.arange(CTX, dtype=jnp.int32)
    queries_four = queries.reshape(CH, RESP, HEADS, HEAD_DIM)
    grads_four = out_grad.reshape(CH, RESP, HEADS, HEAD_DIM)
    causal = rows_all[:, None] <= rows_all[None, :]
    open_sys = jnp.ones((SYS, CH), dtype=bool)

    def visit(carried, response):
        sys_kgrad, sys_vgrad, ctx_kgrad, ctx_vgrad = carried
        owner = parent[response]
        queries_one = queries_four[:, response]
        grads_one = grads_four[:, response]
        live_rows = rows_all < resp_len[response]
        grads_one = jnp.where(live_rows[:, None, None], grads_one, jnp.zeros((), jnp.bfloat16))
        own_keys = resp_key[:, response]
        own_values = resp_value[:, response]
        key_rows = jnp.concatenate([sys_key, ctx_key[owner], own_keys], axis=0)
        value_rows = jnp.concatenate([sys_value, ctx_value[owner], own_values], axis=0)
        ctx_allowed = jnp.broadcast_to((ctx_places < ctx_len[owner])[:, None], (CTX, CH))
        allowed = jnp.concatenate([open_sys, ctx_allowed, causal], axis=0)[:, None, :]
        query_grad, key_grad, value_grad = one_response(queries_one, grads_one, key_rows, value_rows, allowed)
        sys_kgrad = sys_kgrad + key_grad[:SYS]
        sys_vgrad = sys_vgrad + value_grad[:SYS]
        ctx_kgrad = ctx_kgrad.at[owner].add(key_grad[SYS:SYS + CTX])
        ctx_vgrad = ctx_vgrad.at[owner].add(value_grad[SYS:SYS + CTX])
        return (sys_kgrad, sys_vgrad, ctx_kgrad, ctx_vgrad), (query_grad, key_grad[SYS + CTX:], value_grad[SYS + CTX:])

    initial = (jnp.zeros((SYS, HEAD_DIM), jnp.float32), jnp.zeros((SYS, HEAD_DIM), jnp.float32),
               jnp.zeros((CTXS, CTX, HEAD_DIM), jnp.float32), jnp.zeros((CTXS, CTX, HEAD_DIM), jnp.float32))
    finals, gathered = lax.scan(visit, initial, jnp.arange(RESP, dtype=jnp.int32))
    sys_kgrad, sys_vgrad, ctx_kgrad, ctx_vgrad = finals
    query_grads, own_kgrads, own_vgrads = gathered
    d_queries = jnp.transpose(query_grads, (1, 0, 2, 3)).reshape(CH, RESP, HEADS * HEAD_DIM)
    d_resp_key = jnp.transpose(own_kgrads, (1, 0, 2))
    d_resp_value = jnp.transpose(own_vgrads, (1, 0, 2))
    return (d_queries, sys_kgrad, sys_vgrad, ctx_kgrad, ctx_vgrad, d_resp_key, d_resp_value)
```

```python
import functools
import math

import jax
import jax.numpy as jnp
from jax import lax
from jax.experimental import pallas as pl
from jax.experimental.pallas import tpu as pltpu
from jax.sharding import PartitionSpec as P

HEADS = 7
D = 128
NEGATIVE = -1e30
SCALING = D ** (-0.5)
SCALING2 = SCALING * math.log2(math.e)
F32 = jnp.float32
BF16 = jnp.bfloat16
MESH = pl.DeviceIdType.MESH


def nt(a, b):
    return lax.dot_general(a, b, (((1,), (1,)), ((), ())), preferred_element_type=F32)


def tn(a, b):
    return lax.dot_general(a, b, (((0,), (0,)), ((), ())), preferred_element_type=F32)


def nn(a, b):
    return jnp.dot(a, b, preferred_element_type=F32)


def kernel(
    levels, reqs, T, R, SYS, CTX, C, M,
    q_ref, g_ref, rk_ref, rv_ref, sk_ref, sv_ref, ck_ref, cv_ref, parent, rlen, clen,
    dq_ref, dsk_ref, dsv_ref, dck_ref, dcv_ref, drk_ref, drv_ref,
    qf, gf, kvf, kv, shared, ctx_s, q_s, g_s, s_s, p_s, own_part, own_grad, gsend, grecv,
    shared_acc_sys, shared_acc_ctx, csend, crecv, tsend, trecv,
    kv_ss, kv_rs, sh_ss, sh_rs, gr_ss, gr_rs, cs_ss, cs_rs, t_ss, t_rs,
):
    me = lax.axis_index("level")
    mq = lax.axis_index("req")
    SL, CL = SYS // levels, CTX // levels
    K0, V0 = 0, SL + C * CL
    OWN = levels * T

    barrier = pltpu.get_barrier_semaphore()
    for b in range(levels):
        @pl.when(b != me)
        def _(b=b):
            pl.semaphore_signal(barrier, inc=1, device_id=(b, mq), device_id_type=MESH)
    for b in range(reqs):
        @pl.when(b != mq)
        def _(b=b):
            pl.semaphore_signal(barrier, inc=1, device_id=(me, b), device_id_type=MESH)

    mine = pl.ds(pl.multiple_of(me * T, T), T)
    shared[me, K0:K0 + SL] = sk_ref[...]
    shared[me, V0:V0 + SL] = sv_ref[...]
    for c in range(C):
        shared[me, K0 + SL + c * CL:K0 + SL + (c + 1) * CL] = ck_ref[c]
        shared[me, V0 + SL + c * CL:V0 + SL + (c + 1) * CL] = cv_ref[c]
    kvf[0] = rk_ref[...].astype(F32).reshape(T * R, D)
    kvf[1] = rv_ref[...].astype(F32).reshape(T * R, D)
    for r in range(R):
        for i in range(2):
            kv[r, i, mine, :] = kvf[i, pl.ds(r, T, stride=R), :].astype(BF16)
    for b in range(levels):
        @pl.when(b > me)
        def _(b=b):
            kv[:, :, b * T:(b + 1) * T, :] = jnp.zeros((R, 2, T, D), BF16)

    pl.semaphore_wait(barrier, levels + reqs - 2)

    def shared_copy(dst, src):
        return pltpu.make_async_remote_copy(
            src_ref=shared.at[me], dst_ref=shared.at[me],
            send_sem=sh_ss.at[dst], recv_sem=sh_rs.at[src],
            device_id=(dst, mq), device_id_type=MESH)

    def kv_copy(r, dst, src):
        return pltpu.make_async_remote_copy(
            src_ref=kv.at[r, :, mine, :], dst_ref=kv.at[r, :, mine, :],
            send_sem=kv_ss.at[r, dst], recv_sem=kv_rs.at[r, src],
            device_id=(dst, mq), device_id_type=MESH)

    def grad_copy(r, dst, src):
        return pltpu.make_async_remote_copy(
            src_ref=gsend.at[r, dst], dst_ref=grecv.at[r, src],
            send_sem=gr_ss.at[r, dst], recv_sem=gr_rs.at[r, src],
            device_id=(dst, mq), device_id_type=MESH)

    def sum_copy(dst, src):
        return pltpu.make_async_remote_copy(
            src_ref=csend.at[dst], dst_ref=crecv.at[src],
            send_sem=cs_ss.at[dst], recv_sem=cs_rs.at[src],
            device_id=(dst, mq), device_id_type=MESH)

    def total_copy(dst, src):
        return pltpu.make_async_remote_copy(
            src_ref=tsend.at[dst], dst_ref=trecv.at[src],
            send_sem=t_ss.at[dst], recv_sem=t_rs.at[src],
            device_id=(me, dst), device_id_type=MESH)

    for b in range(levels):
        @pl.when(b != me)
        def _(b=b):
            shared_copy(b, me).start()

    def send_keys(r, carry):
        for b in range(levels):
            @pl.when(b > me)
            def _(b=b):
                kv_copy(r, b, me).start()
        return carry

    lax.fori_loop(0, R, send_keys, 0)

    for h in range(HEADS):
        qf[h] = q_ref[:, :, h * D:(h + 1) * D].astype(F32).reshape(T * R, D)
        gf[h] = g_ref[:, :, h * D:(h + 1) * D].astype(F32).reshape(T * R, D)
    row_at = me * T + lax.broadcasted_iota(jnp.int32, (T, D), 0)

    def arrange(r, carry):
        live = row_at < rlen[r]
        rows = pl.ds(r, T, stride=R)
        for h in range(HEADS):
            q_s[r, h * T:(h + 1) * T, :] = qf[h, rows, :].astype(BF16)
            g_s[r, h * T:(h + 1) * T, :] = jnp.where(live, gf[h, rows, :], 0.0).astype(BF16)
        if M > HEADS * T:
            q_s[r, HEADS * T:, :] = jnp.zeros((M - HEADS * T, D), BF16)
            g_s[r, HEADS * T:, :] = jnp.zeros((M - HEADS * T, D), BF16)
        return carry

    lax.fori_loop(0, R, arrange, 0)
    shared_acc_sys[...] = jnp.zeros(shared_acc_sys.shape, F32)
    shared_acc_ctx[...] = jnp.zeros(shared_acc_ctx.shape, F32)
    crecv[me] = jnp.zeros(crecv.shape[1:], BF16)

    for b in range(levels):
        @pl.when(b != me)
        def _(b=b):
            shared_copy(b, b).wait_recv()

    sgroup = min(levels, max(1, 128 // SL))
    cgroup = min(levels, max(1, 128 // CL))
    own_width = min(128, OWN)
    chunks = []
    at = 0
    for b in range(0, levels, sgroup):
        chunks.append(("sys", b, sgroup * SL, at))
        at += sgroup * SL
    for b in range(0, levels, cgroup):
        chunks.append(("ctx", b, cgroup * CL, at))
        at += cgroup * CL
    for b in range(0, OWN, own_width):
        chunks.append(("own", b, own_width, at))
        at += own_width
    row_of_lane = me * T + lax.rem(lax.broadcasted_iota(jnp.int32, (1, M), 1), T)

    def one_response(r, carry):
        for b in range(levels):
            @pl.when(b < me)
            def _(b=b):
                kv_copy(r, b, b).wait_recv()
        where_ctx = parent[r] - mq * C
        limit = jnp.int32(0)
        chosen = []
        for c in range(C):
            chosen.append(jnp.where(where_ctx == c, 1.0, 0.0))
            limit = limit + jnp.where(where_ctx == c, clen[c], 0)
        for which, base in ((0, K0), (1, V0)):
            picked = jnp.zeros((levels, CL, D), F32)
            for c in range(C):
                at = base + SL + c * CL
                picked = picked + chosen[c] * shared[:, at:at + CL, :].astype(F32)
            ctx_s[which] = picked.astype(BF16).reshape(CTX, D)
        q = q_s[r]
        g = g_s[r]

        def rows_of(kind, start, width, which):
            base = (K0, V0)[which]
            if kind == "sys":
                return shared[start:start + sgroup, base:base + SL, :].reshape(width, D)
            if kind == "ctx":
                return ctx_s[which, start * CL:start * CL + width, :]
            return kv[r, which, start:start + width, :]

        tops = jnp.full((8, M), NEGATIVE, F32)
        for kind, start, width, at in chunks:
            scores = nt(rows_of(kind, start, width, 0), q) * SCALING2
            places = lax.broadcasted_iota(jnp.int32, (width, M), 0)
            if kind == "ctx":
                scores = jnp.where(places + start * CL < limit, scores, NEGATIVE)
            if kind == "own":
                scores = jnp.where(places + start <= row_of_lane, scores, NEGATIVE)
            s_s[at:at + width, :] = scores
            tops = jnp.maximum(tops, jnp.max(scores.reshape(width // 8, 8, M), axis=0))
        top = jnp.max(tops, axis=0, keepdims=True)
        totals = jnp.zeros((8, M), F32)
        running = jnp.zeros((8, M), F32)
        for kind, start, width, at in chunks:
            weights = jnp.exp2(s_s[at:at + width, :] - top)
            products = nt(rows_of(kind, start, width, 1), g)
            s_s[at:at + width, :] = weights
            p_s[at:at + width, :] = products
            totals = totals + jnp.sum(weights.reshape(width // 8, 8, M), axis=0)
            running = running + jnp.sum((weights * products).reshape(width // 8, 8, M), axis=0)
        inverse = 1.0 / jnp.sum(totals, axis=0, keepdims=True)
        deltas = jnp.sum(running, axis=0, keepdims=True) * inverse
        dq = jnp.zeros((D, M), F32)
        for kind, start, width, at in chunks:
            chances = s_s[at:at + width, :] * inverse
            slopes = (chances * (p_s[at:at + width, :] - deltas)).astype(BF16)
            dk = nn(slopes, q) * SCALING
            dv = nn(chances.astype(BF16), g)
            dq = dq + tn(rows_of(kind, start, width, 0), slopes)
            if kind == "sys":
                place = slice(start * SL, start * SL + width)
                shared_acc_sys[0, place] += dk
                shared_acc_sys[1, place] += dv
            if kind == "ctx":
                place = slice(start * CL, start * CL + width)
                for c in range(C):
                    shared_acc_ctx[0, c, place] += dk * chosen[c]
                    shared_acc_ctx[1, c, place] += dv * chosen[c]
            if kind == "own":
                own_part[0, start:start + width] = dk
                own_part[1, start:start + width] = dv
        own_grad[r] = own_part[:, mine, :]
        for b in range(levels):
            @pl.when(b < me)
            def _(b=b):
                gsend[r, b] = own_part[:, b * T:(b + 1) * T, :].astype(BF16)
                grad_copy(r, b, me).start()
        dq_rows = jnp.transpose(dq) * SCALING
        for h in range(HEADS):
            qf[h, pl.ds(r, T, stride=R), :] = dq_rows[h * T:(h + 1) * T]
        return carry

    lax.fori_loop(0, R, one_response, 0)

    for b in range(levels):
        @pl.when(b != me)
        def _(b=b):
            for which, base in ((0, K0), (1, V0)):
                csend[b, base:base + SL] = shared_acc_sys[which, b * SL:(b + 1) * SL].astype(BF16)
                for c in range(C):
                    at = base + SL + c * CL
                    csend[b, at:at + CL] = shared_acc_ctx[which, c, b * CL:(b + 1) * CL].astype(BF16)
            sum_copy(b, me).start()

    for h in range(HEADS):
        dq_ref[:, h * D:(h + 1) * D] = qf[h]

    def finish(r, carry):
        for b in range(levels):
            @pl.when(b > me)
            def _(b=b):
                grad_copy(r, b, b).wait_recv()
                own_grad[r] += grecv[r, b].astype(F32)
        rows = pl.ds(r, T, stride=R)
        drk_ref[rows, :] = own_grad[r, 0]
        drv_ref[rows, :] = own_grad[r, 1]
        return carry

    lax.fori_loop(0, R - 1, finish, 0)

    for b in range(levels):
        @pl.when(b != me)
        def _(b=b):
            sum_copy(b, b).wait_recv()
    rq = SL // reqs
    sys_rows = pl.ds(pl.multiple_of(me * SL, SL), SL)
    ctx_rows = pl.ds(pl.multiple_of(me * CL, CL), CL)
    for which, base in ((0, K0), (1, V0)):
        total = shared_acc_sys[which, sys_rows, :]
        for b in range(levels):
            total = total + crecv[b, base:base + SL, :].astype(F32)
        for b in range(reqs):
            tsend[b, which * rq:(which + 1) * rq, :] = total[b * rq:(b + 1) * rq]
    for b in range(reqs):
        @pl.when(b != mq)
        def _(b=b):
            total_copy(b, mq).start()
    trecv[mq] = tsend[mq]
    for which, base, out in ((0, K0, dck_ref), (1, V0, dcv_ref)):
        for c in range(C):
            at = base + SL + c * CL
            total = shared_acc_ctx[which, c, ctx_rows, :]
            for b in range(levels):
                total = total + crecv[b, at:at + CL, :].astype(F32)
            out[c] = total
    finish(R - 1, 0)

    for b in range(levels):
        @pl.when(b != me)
        def _(b=b):
            shared_copy(b, me).wait_send()
            sum_copy(b, me).wait_send()

    def sent(r, carry):
        for b in range(levels):
            @pl.when(b > me)
            def _(b=b):
                kv_copy(r, b, me).wait_send()

            @pl.when(b < me)
            def _(b=b):
                grad_copy(r, b, me).wait_send()
        return carry

    lax.fori_loop(0, R, sent, 0)
    for b in range(reqs):
        @pl.when(b != mq)
        def _(b=b):
            total_copy(b, mq).wait_send()
            total_copy(b, b).wait_recv()
    grand = trecv[0]
    for b in range(1, reqs):
        grand = grand + trecv[b]
    dsk_ref[...] = grand[:rq]
    dsv_ref[...] = grand[rq:]


def shards(levels, reqs, queries, out_grad, resp_key, resp_value, sys_key, sys_value,
           ctx_key, ctx_value, parent, resp_len, ctx_len):
    T, R, _ = queries.shape
    SL, CL, C = sys_key.shape[0], ctx_key.shape[1], ctx_key.shape[0]
    SYS, CTX = SL * levels, CL * levels
    M = -(-HEADS * T // 128) * 128
    OWN = levels * T
    N = SYS + CTX + OWN
    SH = 2 * (SL + C * CL)
    rq = SL // reqs
    vmem = pl.BlockSpec(memory_space=pltpu.VMEM)
    smem = pl.BlockSpec(memory_space=pltpu.SMEM)
    dma = pltpu.SemaphoreType.DMA
    V = pltpu.VMEM
    outs = pl.pallas_call(
        functools.partial(kernel, levels, reqs, T, R, SYS, CTX, C, M),
        out_shape=(
            jax.ShapeDtypeStruct((T * R, HEADS * D), F32),
            jax.ShapeDtypeStruct((rq, D), F32),
            jax.ShapeDtypeStruct((rq, D), F32),
            jax.ShapeDtypeStruct((C, CL, D), F32),
            jax.ShapeDtypeStruct((C, CL, D), F32),
            jax.ShapeDtypeStruct((T * R, D), F32),
            jax.ShapeDtypeStruct((T * R, D), F32),
        ),
        in_specs=[vmem] * 8 + [smem] * 3,
        out_specs=(vmem,) * 7,
        scratch_shapes=[
            V((HEADS, T * R, D), F32),
            V((HEADS, T * R, D), F32),
            V((2, T * R, D), F32),
            V((R, 2, OWN, D), BF16),
            V((levels, SH, D), BF16),
            V((2, CTX, D), BF16),
            V((R, M, D), BF16),
            V((R, M, D), BF16),
            V((N, M), F32),
            V((N, M), F32),
            V((2, OWN, D), F32),
            V((R, 2, T, D), F32),
            V((R, levels, 2, T, D), BF16),
            V((R, levels, 2, T, D), BF16),
            V((2, SYS, D), F32),
            V((2, C, CTX, D), F32),
            V((levels, SH, D), BF16),
            V((levels, SH, D), BF16),
            V((reqs, 2 * rq, D), F32),
            V((reqs, 2 * rq, D), F32),
            dma((R, levels)), dma((R, levels)),
            dma((levels,)), dma((levels,)),
            dma((R, levels)), dma((R, levels)),
            dma((levels,)), dma((levels,)),
            dma((reqs,)), dma((reqs,)),
        ],
        compiler_params=pltpu.CompilerParams(
            collective_id=0, has_side_effects=True, vmem_limit_bytes=48 * 2**20
        ),
        cost_estimate=pl.CostEstimate(
            flops=10 * R * M * N * D, bytes_accessed=10 * T * R * HEADS * D,
            transcendentals=R * M * N,
        ),
    )(queries, out_grad, resp_key, resp_value, sys_key, sys_value, ctx_key, ctx_value,
      parent, resp_len, ctx_len)
    dq, dsk, dsv, dck, dcv, drk, drv = outs
    return (dq.reshape(T, R, HEADS * D), dsk, dsv, dck, dcv,
            drk.reshape(T, R, D), drv.reshape(T, R, D))


def solution(mesh):
    return jax.shard_map(
        functools.partial(shards, mesh.shape["level"], mesh.shape["req"]),
        mesh=mesh,
        in_specs=(
            P("level", "req", None),
            P("level", "req", None),
            P("level", "req", None),
            P("level", "req", None),
            P("level", None),
            P("level", None),
            P("req", "level", None),
            P("req", "level", None),
            P("req"),
            P("req"),
            P("req"),
        ),
        out_specs=(
            P("level", "req", None),
            P(("level", "req"), None),
            P(("level", "req"), None),
            P("req", "level", None),
            P("req", "level", None),
            P("level", "req", None),
            P("level", "req", None),
        ),
        check_vma=False,
    )
```

```python
import functools
import math

import jax
import jax.numpy as jnp
from jax import lax
from jax.experimental import pallas as pl
from jax.experimental.pallas import tpu as pltpu
from jax.sharding import PartitionSpec as P

HEADS = 7
D = 128
NEGATIVE = -1e30
SCALING = D ** (-0.5)
SCALING2 = SCALING * math.log2(math.e)
F32 = jnp.float32
BF16 = jnp.bfloat16
MESH = pl.DeviceIdType.MESH


def nt(a, b):
    return lax.dot_general(a, b, (((1,), (1,)), ((), ())), preferred_element_type=F32)


def tn(a, b):
    return lax.dot_general(a, b, (((0,), (0,)), ((), ())), preferred_element_type=F32)


def nn(a, b):
    return jnp.dot(a, b, preferred_element_type=F32)


def kernel(
    levels, reqs, T, R, SYS, CTX, C, M,
    q_in, g_in, rk_in, rv_in, sk_in, sv_in, ck_in, cv_in, parent_in, rlen_in, clen_in,
    dq_out, dsk_ref, dsv_ref, dck_ref, dcv_ref, drk_ref, drv_ref,
    q_ref, g_ref, rk_ref, rv_ref, parent, rlen, clen, in_s, dq_ref, dq_s, qf, gf, kvf, kv, shared, ctx_s, q_s, g_s, s_s, p_s, own_part, own_grad, gsend, grecv,
    shared_acc_sys, shared_acc_ctx, csend, crecv, tsend, trecv,
    kv_ss, kv_rs, sh_ss, sh_rs, gr_ss, gr_rs, cs_ss, cs_rs, t_ss, t_rs,
):
    me = lax.axis_index("level")
    mq = lax.axis_index("req")
    SL, CL = SYS // levels, CTX // levels
    K0, V0 = 0, SL + C * CL
    OWN = levels * T

    barrier = pltpu.get_barrier_semaphore()
    for b in range(levels):
        @pl.when(b != me)
        def _(b=b):
            pl.semaphore_signal(barrier, inc=1, device_id=(b, mq), device_id_type=MESH)
    for b in range(reqs):
        @pl.when(b != mq)
        def _(b=b):
            pl.semaphore_signal(barrier, inc=1, device_id=(me, b), device_id_type=MESH)

    loads = []

    def load(src, dst):
        copy = pltpu.make_async_copy(src, dst, in_s.at[len(loads)])
        copy.start()
        loads.append(copy)

    load(rk_in, rk_ref)
    load(rv_in, rv_ref)
    load(sk_in, shared.at[me, K0:K0 + SL])
    load(sv_in, shared.at[me, V0:V0 + SL])
    for c in range(C):
        load(ck_in.at[c], shared.at[me, K0 + SL + c * CL:K0 + SL + (c + 1) * CL])
        load(cv_in.at[c], shared.at[me, V0 + SL + c * CL:V0 + SL + (c + 1) * CL])
    first = len(loads)
    load(q_in, q_ref)
    load(g_in, g_ref)
    load(parent_in, parent)
    load(rlen_in, rlen)
    load(clen_in, clen)

    mine = pl.ds(pl.multiple_of(me * T, T), T)
    for copy in loads[:2]:
        copy.wait()
    kvf[0] = rk_ref[...].astype(F32).reshape(T * R, D)
    kvf[1] = rv_ref[...].astype(F32).reshape(T * R, D)
    for r in range(R):
        for i in range(2):
            kv[r, i, mine, :] = kvf[i, pl.ds(r, T, stride=R), :].astype(BF16)
    for b in range(levels):
        @pl.when(b > me)
        def _(b=b):
            kv[:, :, b * T:(b + 1) * T, :] = jnp.zeros((R, 2, T, D), BF16)

    for copy in loads[2:first]:
        copy.wait()
    pl.semaphore_wait(barrier, levels + reqs - 2)

    def shared_copy(dst, src):
        return pltpu.make_async_remote_copy(
            src_ref=shared.at[me], dst_ref=shared.at[me],
            send_sem=sh_ss.at[dst], recv_sem=sh_rs.at[src],
            device_id=(dst, mq), device_id_type=MESH)

    def kv_copy(r, dst, src):
        return pltpu.make_async_remote_copy(
            src_ref=kv.at[r, :, mine, :], dst_ref=kv.at[r, :, mine, :],
            send_sem=kv_ss.at[r, dst], recv_sem=kv_rs.at[r, src],
            device_id=(dst, mq), device_id_type=MESH)

    def grad_copy(r, dst, src):
        return pltpu.make_async_remote_copy(
            src_ref=gsend.at[r, dst], dst_ref=grecv.at[r, src],
            send_sem=gr_ss.at[r, dst], recv_sem=gr_rs.at[r, src],
            device_id=(dst, mq), device_id_type=MESH)

    def sum_copy(dst, src):
        return pltpu.make_async_remote_copy(
            src_ref=csend.at[dst], dst_ref=crecv.at[src],
            send_sem=cs_ss.at[dst], recv_sem=cs_rs.at[src],
            device_id=(dst, mq), device_id_type=MESH)

    def total_copy(dst, src):
        return pltpu.make_async_remote_copy(
            src_ref=tsend.at[dst], dst_ref=trecv.at[src],
            send_sem=t_ss.at[dst], recv_sem=t_rs.at[src],
            device_id=(me, dst), device_id_type=MESH)

    for b in range(levels):
        @pl.when(b != me)
        def _(b=b):
            shared_copy(b, me).start()

    def send_keys(r, carry):
        for b in range(levels):
            @pl.when(b > me)
            def _(b=b):
                kv_copy(r, b, me).start()
        return carry

    lax.fori_loop(0, R, send_keys, 0)

    for copy in loads[first:]:
        copy.wait()
    for h in range(HEADS):
        qf[h] = q_ref[:, :, h * D:(h + 1) * D].astype(F32).reshape(T * R, D)
        gf[h] = g_ref[:, :, h * D:(h + 1) * D].astype(F32).reshape(T * R, D)
    row_at = me * T + lax.broadcasted_iota(jnp.int32, (T, D), 0)

    def arrange(r, carry):
        live = row_at < rlen[r]
        rows = pl.ds(r, T, stride=R)
        for h in range(HEADS):
            q_s[r, h * T:(h + 1) * T, :] = qf[h, rows, :].astype(BF16)
            g_s[r, h * T:(h + 1) * T, :] = jnp.where(live, gf[h, rows, :], 0.0).astype(BF16)
        if M > HEADS * T:
            q_s[r, HEADS * T:, :] = jnp.zeros((M - HEADS * T, D), BF16)
            g_s[r, HEADS * T:, :] = jnp.zeros((M - HEADS * T, D), BF16)
        return carry

    lax.fori_loop(0, R, arrange, 0)
    shared_acc_sys[...] = jnp.zeros(shared_acc_sys.shape, F32)
    shared_acc_ctx[...] = jnp.zeros(shared_acc_ctx.shape, F32)
    crecv[me] = jnp.zeros(crecv.shape[1:], BF16)

    for b in range(levels):
        @pl.when(b != me)
        def _(b=b):
            shared_copy(b, b).wait_recv()

    sgroup = min(levels, max(1, 128 // SL))
    cgroup = min(levels, max(1, 128 // CL))
    own_width = min(128, OWN)
    chunks = []
    at = 0
    for b in range(0, levels, sgroup):
        chunks.append(("sys", b, sgroup * SL, at))
        at += sgroup * SL
    for b in range(0, levels, cgroup):
        chunks.append(("ctx", b, cgroup * CL, at))
        at += cgroup * CL
    for b in range(0, OWN, own_width):
        chunks.append(("own", b, own_width, at))
        at += own_width
    row_of_lane = me * T + lax.rem(lax.broadcasted_iota(jnp.int32, (1, M), 1), T)

    def one_response(r, carry):
        for b in range(levels):
            @pl.when(b < me)
            def _(b=b):
                kv_copy(r, b, b).wait_recv()
        where_ctx = parent[r] - mq * C
        limit = jnp.int32(0)
        chosen = []
        for c in range(C):
            chosen.append(jnp.where(where_ctx == c, 1.0, 0.0))
            limit = limit + jnp.where(where_ctx == c, clen[c], 0)
        for which, base in ((0, K0), (1, V0)):
            picked = jnp.zeros((levels, CL, D), F32)
            for c in range(C):
                at = base + SL + c * CL
                picked = picked + chosen[c] * shared[:, at:at + CL, :].astype(F32)
            ctx_s[which] = picked.astype(BF16).reshape(CTX, D)
        q = q_s[r]
        g = g_s[r]

        def rows_of(kind, start, width, which):
            base = (K0, V0)[which]
            if kind == "sys":
                return shared[start:start + sgroup, base:base + SL, :].reshape(width, D)
            if kind == "ctx":
                return ctx_s[which, start * CL:start * CL + width, :]
            return kv[r, which, start:start + width, :]

        tops = jnp.full((8, M), NEGATIVE, F32)
        for kind, start, width, at in chunks:
            scores = nt(rows_of(kind, start, width, 0), q) * SCALING2
            places = lax.broadcasted_iota(jnp.int32, (width, M), 0)
            if kind == "ctx":
                scores = jnp.where(places + start * CL < limit, scores, NEGATIVE)
            if kind == "own":
                scores = jnp.where(places + start <= row_of_lane, scores, NEGATIVE)
            s_s[at:at + width, :] = scores
            tops = jnp.maximum(tops, jnp.max(scores.reshape(width // 8, 8, M), axis=0))
        top = jnp.max(tops, axis=0, keepdims=True)
        totals = jnp.zeros((8, M), F32)
        running = jnp.zeros((8, M), F32)
        for kind, start, width, at in chunks:
            weights = jnp.exp2(s_s[at:at + width, :] - top)
            products = nt(rows_of(kind, start, width, 1), g)
            s_s[at:at + width, :] = weights
            p_s[at:at + width, :] = products
            totals = totals + jnp.sum(weights.reshape(width // 8, 8, M), axis=0)
            running = running + jnp.sum((weights * products).reshape(width // 8, 8, M), axis=0)
        inverse = 1.0 / jnp.sum(totals, axis=0, keepdims=True)
        deltas = jnp.sum(running, axis=0, keepdims=True) * inverse
        dq = jnp.zeros((D, M), F32)
        for kind, start, width, at in chunks:
            chances = s_s[at:at + width, :] * inverse
            slopes = (chances * (p_s[at:at + width, :] - deltas)).astype(BF16)
            dk = nn(slopes, q) * SCALING
            dv = nn(chances.astype(BF16), g)
            dq = dq + tn(rows_of(kind, start, width, 0), slopes)
            if kind == "sys":
                place = slice(start * SL, start * SL + width)
                shared_acc_sys[0, place] += dk
                shared_acc_sys[1, place] += dv
            if kind == "ctx":
                place = slice(start * CL, start * CL + width)
                for c in range(C):
                    shared_acc_ctx[0, c, place] += dk * chosen[c]
                    shared_acc_ctx[1, c, place] += dv * chosen[c]
            if kind == "own":
                own_part[0, start:start + width] = dk
                own_part[1, start:start + width] = dv
        own_grad[r] = own_part[:, mine, :]
        for b in range(levels):
            @pl.when(b < me)
            def _(b=b):
                gsend[r, b] = own_part[:, b * T:(b + 1) * T, :].astype(BF16)
                grad_copy(r, b, me).start()
        dq_rows = jnp.transpose(dq) * SCALING
        for h in range(HEADS):
            dq_ref[h, pl.ds(r, T, stride=R), :] = dq_rows[h * T:(h + 1) * T]
        return carry

    lax.fori_loop(0, R, one_response, 0)
    dq_copy = pltpu.make_async_copy(dq_ref, dq_out, dq_s)
    dq_copy.start()

    for b in range(levels):
        @pl.when(b != me)
        def _(b=b):
            for which, base in ((0, K0), (1, V0)):
                csend[b, base:base + SL] = shared_acc_sys[which, b * SL:(b + 1) * SL].astype(BF16)
                for c in range(C):
                    at = base + SL + c * CL
                    csend[b, at:at + CL] = shared_acc_ctx[which, c, b * CL:(b + 1) * CL].astype(BF16)
            sum_copy(b, me).start()

    def finish(r, carry):
        for b in range(levels):
            @pl.when(b > me)
            def _(b=b):
                grad_copy(r, b, b).wait_recv()
                own_grad[r] += grecv[r, b].astype(F32)
        rows = pl.ds(r, T, stride=R)
        drk_ref[rows, :] = own_grad[r, 0]
        drv_ref[rows, :] = own_grad[r, 1]
        return carry

    lax.fori_loop(0, R - 1, finish, 0)

    for b in range(levels):
        @pl.when(b != me)
        def _(b=b):
            sum_copy(b, b).wait_recv()
    rq = SL // reqs
    sys_rows = pl.ds(pl.multiple_of(me * SL, SL), SL)
    ctx_rows = pl.ds(pl.multiple_of(me * CL, CL), CL)
    for which, base in ((0, K0), (1, V0)):
        total = shared_acc_sys[which, sys_rows, :]
        for b in range(levels):
            total = total + crecv[b, base:base + SL, :].astype(F32)
        for b in range(reqs):
            tsend[b, which * rq:(which + 1) * rq, :] = total[b * rq:(b + 1) * rq]
    for b in range(reqs):
        @pl.when(b != mq)
        def _(b=b):
            total_copy(b, mq).start()
    trecv[mq] = tsend[mq]
    for which, base, out in ((0, K0, dck_ref), (1, V0, dcv_ref)):
        for c in range(C):
            at = base + SL + c * CL
            total = shared_acc_ctx[which, c, ctx_rows, :]
            for b in range(levels):
                total = total + crecv[b, at:at + CL, :].astype(F32)
            out[c] = total
    finish(R - 1, 0)

    for b in range(levels):
        @pl.when(b != me)
        def _(b=b):
            shared_copy(b, me).wait_send()
            sum_copy(b, me).wait_send()

    def sent(r, carry):
        for b in range(levels):
            @pl.when(b > me)
            def _(b=b):
                kv_copy(r, b, me).wait_send()

            @pl.when(b < me)
            def _(b=b):
                grad_copy(r, b, me).wait_send()
        return carry

    lax.fori_loop(0, R, sent, 0)
    for b in range(reqs):
        @pl.when(b != mq)
        def _(b=b):
            total_copy(b, mq).wait_send()
            total_copy(b, b).wait_recv()
    dq_copy.wait()
    grand = trecv[0]
    for b in range(1, reqs):
        grand = grand + trecv[b]
    dsk_ref[...] = grand[:rq]
    dsv_ref[...] = grand[rq:]


def write_out(*refs):
    ins, outs, sems = refs[:7], refs[7:14], refs[14]
    pairs = [(ins[0].at[h], outs[0].at[:, :, h * D:(h + 1) * D]) for h in range(HEADS)]
    pairs += list(zip(ins[1:], outs[1:]))
    copies = [
        pltpu.make_async_copy(src, dst, sems.at[i]) for i, (src, dst) in enumerate(pairs)
    ]
    for copy in copies:
        copy.start()
    for copy in copies:
        copy.wait()


def shards(levels, reqs, queries, out_grad, resp_key, resp_value, sys_key, sys_value,
           ctx_key, ctx_value, parent, resp_len, ctx_len):
    T, R, _ = queries.shape
    SL, CL, C = sys_key.shape[0], ctx_key.shape[1], ctx_key.shape[0]
    SYS, CTX = SL * levels, CL * levels
    M = -(-HEADS * T // 128) * 128
    OWN = levels * T
    N = SYS + CTX + OWN
    SH = 2 * (SL + C * CL)
    rq = SL // reqs
    vmem = pl.BlockSpec(memory_space=pltpu.VMEM)
    any_place = pl.BlockSpec(memory_space=pl.ANY)
    dma = pltpu.SemaphoreType.DMA
    V = pltpu.VMEM
    outs = pl.pallas_call(
        functools.partial(kernel, levels, reqs, T, R, SYS, CTX, C, M),
        out_shape=(
            jax.ShapeDtypeStruct((HEADS, T * R, D), F32),
            jax.ShapeDtypeStruct((rq, D), F32),
            jax.ShapeDtypeStruct((rq, D), F32),
            jax.ShapeDtypeStruct((C, CL, D), F32),
            jax.ShapeDtypeStruct((C, CL, D), F32),
            jax.ShapeDtypeStruct((T * R, D), F32),
            jax.ShapeDtypeStruct((T * R, D), F32),
        ),
        in_specs=[any_place] * 11,
        out_specs=(any_place,) + (vmem,) * 6,
        scratch_shapes=[
            V((T, R, HEADS * D), BF16),
            V((T, R, HEADS * D), BF16),
            V((T, R, D), BF16),
            V((T, R, D), BF16),
            pltpu.SMEM((R,), jnp.int32),
            pltpu.SMEM((R,), jnp.int32),
            pltpu.SMEM((C,), jnp.int32),
            dma((9 + 2 * C,)),
            V((HEADS, T * R, D), F32),
            dma(()),
            V((HEADS, T * R, D), F32),
            V((HEADS, T * R, D), F32),
            V((2, T * R, D), F32),
            V((R, 2, OWN, D), BF16),
            V((levels, SH, D), BF16),
            V((2, CTX, D), BF16),
            V((R, M, D), BF16),
            V((R, M, D), BF16),
            V((N, M), F32),
            V((N, M), F32),
            V((2, OWN, D), F32),
            V((R, 2, T, D), F32),
            V((R, levels, 2, T, D), BF16),
            V((R, levels, 2, T, D), BF16),
            V((2, SYS, D), F32),
            V((2, C, CTX, D), F32),
            V((levels, SH, D), BF16),
            V((levels, SH, D), BF16),
            V((reqs, 2 * rq, D), F32),
            V((reqs, 2 * rq, D), F32),
            dma((R, levels)), dma((R, levels)),
            dma((levels,)), dma((levels,)),
            dma((R, levels)), dma((R, levels)),
            dma((levels,)), dma((levels,)),
            dma((reqs,)), dma((reqs,)),
        ],
        compiler_params=pltpu.CompilerParams(
            collective_id=0, has_side_effects=True, vmem_limit_bytes=56 * 2**20
        ),
        cost_estimate=pl.CostEstimate(
            flops=10 * R * M * N * D, bytes_accessed=10 * T * R * HEADS * D,
            transcendentals=R * M * N,
        ),
    )(queries, out_grad, resp_key, resp_value, sys_key, sys_value, ctx_key, ctx_value,
      parent, resp_len, ctx_len)
    dq, dsk, dsv, dck, dcv, drk, drv = outs
    finals = (dq.reshape(HEADS, T, R, D), dsk, dsv, dck, dcv,
              drk.reshape(T, R, D), drv.reshape(T, R, D))
    shapes = ((T, R, HEADS * D),) + tuple(a.shape for a in finals[1:])
    return pl.pallas_call(
        write_out,
        out_shape=tuple(jax.ShapeDtypeStruct(shape, F32) for shape in shapes),
        in_specs=[any_place] * 7,
        out_specs=(any_place,) * 7,
        scratch_shapes=[dma((HEADS + 6,))],
        compiler_params=pltpu.CompilerParams(vmem_limit_bytes=56 * 2**20),
    )(*finals)


def solution(mesh):
    return jax.shard_map(
        functools.partial(shards, mesh.shape["level"], mesh.shape["req"]),
        mesh=mesh,
        in_specs=(
            P("level", "req", None),
            P("level", "req", None),
            P("level", "req", None),
            P("level", "req", None),
            P("level", None),
            P("level", None),
            P("req", "level", None),
            P("req", "level", None),
            P("req"),
            P("req"),
            P("req"),
        ),
        out_specs=(
            P("level", "req", None),
            P(("level", "req"), None),
            P(("level", "req"), None),
            P("req", "level", None),
            P("req", "level", None),
            P("level", "req", None),
            P("level", "req", None),
        ),
        check_vma=False,
    )
```

```python
import functools
import math

import jax
import jax.numpy as jnp
from jax import lax
from jax.experimental import pallas as pl
from jax.experimental.pallas import tpu as pltpu
from jax.sharding import PartitionSpec as P

HEADS = 7
D = 128
NEGATIVE = -1e30
SCALING = D ** (-0.5)
SCALING2 = SCALING * math.log2(math.e)
F32 = jnp.float32
BF16 = jnp.bfloat16
MESH = pl.DeviceIdType.MESH


def nt(a, b):
    return lax.dot_general(a, b, (((1,), (1,)), ((), ())), preferred_element_type=F32)


def tn(a, b):
    return lax.dot_general(a, b, (((0,), (0,)), ((), ())), preferred_element_type=F32)


def nn(a, b):
    return jnp.dot(a, b, preferred_element_type=F32)


def kernel(
    levels, reqs, T, R, SYS, CTX, C, M, PAIR,
    q_in, g_in, rk_in, rv_in, sk_in, sv_in, ck_in, cv_in, parent_in, rlen_in, clen_in,
    dq_out, dsk_ref, dsv_ref, dck_ref, dcv_ref, drk_ref, drv_ref,
    q_ref, g_ref, rk_ref, rv_ref, parent, rlen, clen, in_s, dq_ref, dq_s, qf, gf, kvf, kv, shared, keys, q_s, g_s, s_s, p_s, ch_s, sl_s, own_part, own_grad, gsend, grecv,
    shared_acc_sys, shared_acc_ctx, csend, crecv, tsend, trecv,
    kv_ss, kv_rs, sh_ss, sh_rs, gr_ss, gr_rs, cs_ss, cs_rs, t_ss, t_rs,
):
    me = lax.axis_index("level")
    mq = lax.axis_index("req")
    SL, CL = SYS // levels, CTX // levels
    K0, V0 = 0, SL + C * CL
    OWN = levels * T

    barrier = pltpu.get_barrier_semaphore()
    for b in range(levels):
        @pl.when(b != me)
        def _(b=b):
            pl.semaphore_signal(barrier, inc=1, device_id=(b, mq), device_id_type=MESH)
    for b in range(reqs):
        @pl.when(b != mq)
        def _(b=b):
            pl.semaphore_signal(barrier, inc=1, device_id=(me, b), device_id_type=MESH)

    loads = []

    def load(src, dst):
        copy = pltpu.make_async_copy(src, dst, in_s.at[len(loads)])
        copy.start()
        loads.append(copy)

    load(rk_in, rk_ref)
    load(rv_in, rv_ref)
    load(sk_in, shared.at[me, K0:K0 + SL])
    load(sv_in, shared.at[me, V0:V0 + SL])
    for c in range(C):
        load(ck_in.at[c], shared.at[me, K0 + SL + c * CL:K0 + SL + (c + 1) * CL])
        load(cv_in.at[c], shared.at[me, V0 + SL + c * CL:V0 + SL + (c + 1) * CL])
    first = len(loads)
    load(q_in, q_ref)
    load(g_in, g_ref)
    load(parent_in, parent)
    load(rlen_in, rlen)
    load(clen_in, clen)

    mine = pl.ds(pl.multiple_of(me * T, T), T)
    for copy in loads[:2]:
        copy.wait()
    kvf[0] = rk_ref[...].astype(F32).reshape(T * R, D)
    kvf[1] = rv_ref[...].astype(F32).reshape(T * R, D)
    for r in range(R):
        for i in range(2):
            kv[r, i, mine, :] = kvf[i, pl.ds(r, T, stride=R), :].astype(BF16)
    for b in range(levels):
        @pl.when(b > me)
        def _(b=b):
            kv[:, :, b * T:(b + 1) * T, :] = jnp.zeros((R, 2, T, D), BF16)

    for copy in loads[2:first]:
        copy.wait()
    pl.semaphore_wait(barrier, levels + reqs - 2)

    def shared_copy(dst, src):
        return pltpu.make_async_remote_copy(
            src_ref=shared.at[me], dst_ref=shared.at[me],
            send_sem=sh_ss.at[dst], recv_sem=sh_rs.at[src],
            device_id=(dst, mq), device_id_type=MESH)

    def kv_copy(r, dst, src):
        return pltpu.make_async_remote_copy(
            src_ref=kv.at[r, :, mine, :], dst_ref=kv.at[r, :, mine, :],
            send_sem=kv_ss.at[r, dst], recv_sem=kv_rs.at[r, src],
            device_id=(dst, mq), device_id_type=MESH)

    def grad_copy(r, dst, src):
        return pltpu.make_async_remote_copy(
            src_ref=gsend.at[r, dst], dst_ref=grecv.at[r, src],
            send_sem=gr_ss.at[r, dst], recv_sem=gr_rs.at[r, src],
            device_id=(dst, mq), device_id_type=MESH)

    def sum_copy(dst, src):
        return pltpu.make_async_remote_copy(
            src_ref=csend.at[dst], dst_ref=crecv.at[src],
            send_sem=cs_ss.at[dst], recv_sem=cs_rs.at[src],
            device_id=(dst, mq), device_id_type=MESH)

    def total_copy(dst, src):
        return pltpu.make_async_remote_copy(
            src_ref=tsend.at[dst], dst_ref=trecv.at[src],
            send_sem=t_ss.at[dst], recv_sem=t_rs.at[src],
            device_id=(me, dst), device_id_type=MESH)

    for b in range(levels):
        @pl.when(b != me)
        def _(b=b):
            shared_copy(b, me).start()

    def send_keys(r, carry):
        for b in range(levels):
            @pl.when(b > me)
            def _(b=b):
                kv_copy(r, b, me).start()
        return carry

    lax.fori_loop(0, R, send_keys, 0)

    for copy in loads[first:]:
        copy.wait()
    for h in range(HEADS):
        qf[h] = q_ref[:, :, h * D:(h + 1) * D].astype(F32).reshape(T * R, D)
        gf[h] = g_ref[:, :, h * D:(h + 1) * D].astype(F32).reshape(T * R, D)
    row_at = me * T + lax.broadcasted_iota(jnp.int32, (T, D), 0)

    def arrange(r, carry):
        live = row_at < rlen[r]
        rows = pl.ds(r, T, stride=R)
        for h in range(HEADS):
            q_s[r, h * T:(h + 1) * T, :] = qf[h, rows, :].astype(BF16)
            g_s[r, h * T:(h + 1) * T, :] = jnp.where(live, gf[h, rows, :], 0.0).astype(BF16)
        if M > HEADS * T:
            q_s[r, HEADS * T:, :] = jnp.zeros((M - HEADS * T, D), BF16)
            g_s[r, HEADS * T:, :] = jnp.zeros((M - HEADS * T, D), BF16)
        return carry

    lax.fori_loop(0, R, arrange, 0)
    shared_acc_sys[...] = jnp.zeros(shared_acc_sys.shape, F32)
    shared_acc_ctx[...] = jnp.zeros(shared_acc_ctx.shape, F32)
    crecv[me] = jnp.zeros(crecv.shape[1:], BF16)

    for b in range(levels):
        @pl.when(b != me)
        def _(b=b):
            shared_copy(b, b).wait_recv()

    chunks = []
    for kind, begin, length in (("sys", 0, SYS), ("ctx", SYS, CTX), ("own", SYS + CTX, OWN)):
        width = min(128, length)
        for start in range(0, length, width):
            chunks.append((kind, start, width, slice(begin + start, begin + start + width)))
    row_of_lane = me * T + lax.rem(lax.broadcasted_iota(jnp.int32, (1, M), 1), T)
    for j in range(PAIR):
        for i, base in ((0, K0), (1, V0)):
            keys[j, i, :SYS, :] = shared[:, base:base + SL, :].reshape(SYS, D)

    def prepare(j, r):
        where_ctx = parent[r] - mq * C
        limit = jnp.int32(0)
        chosen = []
        for c in range(C):
            chosen.append(jnp.where(where_ctx == c, 1.0, 0.0))
            limit = limit + jnp.where(where_ctx == c, clen[c], 0)
        for i, base in ((0, K0), (1, V0)):
            picked = jnp.zeros((levels, CL, D), F32)
            for c in range(C):
                at = base + SL + c * CL
                picked = picked + chosen[c] * shared[:, at:at + CL, :].astype(F32)
            keys[j, i, SYS:SYS + CTX, :] = picked.astype(BF16).reshape(CTX, D)
            keys[j, i, SYS + CTX:, :] = kv[r, i]
        s_s[j] = nt(keys[j, 0], q_s[r])
        p_s[j] = nt(keys[j, 1], g_s[r])
        return chosen, limit

    def maxima(j, limit):
        tops = jnp.full((8, M), NEGATIVE, F32)
        for kind, start, width, at in chunks:
            scores = s_s[j, at, :] * SCALING2
            places = lax.broadcasted_iota(jnp.int32, (width, M), 0)
            if kind == "ctx":
                scores = jnp.where(places < limit - start, scores, NEGATIVE)
            if kind == "own":
                scores = jnp.where(places <= row_of_lane - start, scores, NEGATIVE)
            if kind != "sys":
                s_s[j, at, :] = scores
            tops = jnp.maximum(tops, jnp.max(scores.reshape(width // 8, 8, M), axis=0))
        return jnp.max(tops, axis=0, keepdims=True)

    def sums(j, top):
        totals = jnp.zeros((8, M), F32)
        running = jnp.zeros((8, M), F32)
        for kind, start, width, at in chunks:
            scores = s_s[j, at, :]
            if kind == "sys":
                scores = scores * SCALING2
            weights = jnp.exp2(scores - top)
            s_s[j, at, :] = weights
            totals = totals + jnp.sum(weights.reshape(width // 8, 8, M), axis=0)
            parts = weights * p_s[j, at, :]
            running = running + jnp.sum(parts.reshape(width // 8, 8, M), axis=0)
        inverse = 1.0 / jnp.sum(totals, axis=0, keepdims=True)
        return inverse, jnp.sum(running, axis=0, keepdims=True) * inverse

    def roundings(j, inverse, deltas):
        for kind, start, width, at in chunks:
            chances = s_s[j, at, :] * inverse
            ch_s[j, at, :] = chances.astype(BF16)
            sl_s[j, at, :] = (chances * (p_s[j, at, :] - deltas)).astype(BF16)

    def gradients(j, r, chosen):
        dk = nn(sl_s[j], q_s[r]) * SCALING
        dv = nn(ch_s[j], g_s[r])
        for i, grad in ((0, dk), (1, dv)):
            shared_acc_sys[i] += grad[:SYS]
            for c in range(C):
                shared_acc_ctx[i, c] += grad[SYS:SYS + CTX] * chosen[c]
            own_part[j, i] = grad[SYS + CTX:]
        dq_rows = jnp.transpose(tn(keys[j, 0], sl_s[j])) * SCALING
        for h in range(HEADS):
            dq_ref[h, pl.ds(r, T, stride=R), :] = dq_rows[h * T:(h + 1) * T]

    def responses(step, carry):
        rs = [step * PAIR + j for j in range(PAIR)]
        for b in range(levels):
            @pl.when(b < me)
            def _(b=b):
                for r in rs:
                    kv_copy(r, b, b).wait_recv()
        ready = [prepare(j, r) for j, r in enumerate(rs)]
        tops = [maxima(j, ready[j][1]) for j in range(PAIR)]
        for j, r in enumerate(rs):
            roundings(j, *sums(j, tops[j]))
        for j, r in enumerate(rs):
            gradients(j, r, ready[j][0])
        for j, r in enumerate(rs):
            own_grad[r] = own_part[j, :, mine, :]
        for b in range(levels):
            @pl.when(b < me)
            def _(b=b):
                for j, r in enumerate(rs):
                    gsend[r, b] = own_part[j, :, b * T:(b + 1) * T, :].astype(BF16)
                    grad_copy(r, b, me).start()
        return carry

    lax.fori_loop(0, R // PAIR, responses, 0)
    dq_copy = pltpu.make_async_copy(dq_ref, dq_out, dq_s)
    dq_copy.start()

    for b in range(levels):
        @pl.when(b != me)
        def _(b=b):
            for which, base in ((0, K0), (1, V0)):
                csend[b, base:base + SL] = shared_acc_sys[which, b * SL:(b + 1) * SL].astype(BF16)
                for c in range(C):
                    at = base + SL + c * CL
                    csend[b, at:at + CL] = shared_acc_ctx[which, c, b * CL:(b + 1) * CL].astype(BF16)
            sum_copy(b, me).start()

    def finish(r, carry):
        for b in range(levels):
            @pl.when(b > me)
            def _(b=b):
                grad_copy(r, b, b).wait_recv()
                own_grad[r] += grecv[r, b].astype(F32)
        rows = pl.ds(r, T, stride=R)
        drk_ref[rows, :] = own_grad[r, 0]
        drv_ref[rows, :] = own_grad[r, 1]
        return carry

    lax.fori_loop(0, R - 1, finish, 0)

    for b in range(levels):
        @pl.when(b != me)
        def _(b=b):
            sum_copy(b, b).wait_recv()
    rq = SL // reqs
    sys_rows = pl.ds(pl.multiple_of(me * SL, SL), SL)
    ctx_rows = pl.ds(pl.multiple_of(me * CL, CL), CL)
    for which, base in ((0, K0), (1, V0)):
        total = shared_acc_sys[which, sys_rows, :]
        for b in range(levels):
            total = total + crecv[b, base:base + SL, :].astype(F32)
        for b in range(reqs):
            tsend[b, which * rq:(which + 1) * rq, :] = total[b * rq:(b + 1) * rq]
    for b in range(reqs):
        @pl.when(b != mq)
        def _(b=b):
            total_copy(b, mq).start()
    trecv[mq] = tsend[mq]
    for which, base, out in ((0, K0, dck_ref), (1, V0, dcv_ref)):
        for c in range(C):
            at = base + SL + c * CL
            total = shared_acc_ctx[which, c, ctx_rows, :]
            for b in range(levels):
                total = total + crecv[b, at:at + CL, :].astype(F32)
            out[c] = total
    finish(R - 1, 0)

    for b in range(levels):
        @pl.when(b != me)
        def _(b=b):
            shared_copy(b, me).wait_send()
            sum_copy(b, me).wait_send()

    def sent(r, carry):
        for b in range(levels):
            @pl.when(b > me)
            def _(b=b):
                kv_copy(r, b, me).wait_send()

            @pl.when(b < me)
            def _(b=b):
                grad_copy(r, b, me).wait_send()
        return carry

    lax.fori_loop(0, R, sent, 0)
    for b in range(reqs):
        @pl.when(b != mq)
        def _(b=b):
            total_copy(b, mq).wait_send()
            total_copy(b, b).wait_recv()
    dq_copy.wait()
    grand = trecv[0]
    for b in range(1, reqs):
        grand = grand + trecv[b]
    dsk_ref[...] = grand[:rq]
    dsv_ref[...] = grand[rq:]


def write_out(*refs):
    ins, outs, held, sem_in, sem_out = refs[:7], refs[7:14], refs[14:21], refs[21], refs[22]
    pieces = [(ins[0].at[h], held[0].at[h], outs[0].at[:, :, h * D:(h + 1) * D])
              for h in range(HEADS)]
    pieces += list(zip(ins[1:], held[1:], outs[1:]))
    reads = [pltpu.make_async_copy(src, mid, sem_in.at[i])
             for i, (src, mid, _) in enumerate(pieces)]
    writes = [pltpu.make_async_copy(mid, dst, sem_out.at[i])
              for i, (_, mid, dst) in enumerate(pieces)]
    for copy in reads:
        copy.start()
    for read, write in zip(reads, writes):
        read.wait()
        write.start()
    for copy in writes:
        copy.wait()


def shards(levels, reqs, queries, out_grad, resp_key, resp_value, sys_key, sys_value,
           ctx_key, ctx_value, parent, resp_len, ctx_len):
    T, R, _ = queries.shape
    SL, CL, C = sys_key.shape[0], ctx_key.shape[1], ctx_key.shape[0]
    SYS, CTX = SL * levels, CL * levels
    M = -(-HEADS * T // 128) * 128
    OWN = levels * T
    PAIR = 2 if R % 2 == 0 else 1
    N = SYS + CTX + OWN
    SH = 2 * (SL + C * CL)
    rq = SL // reqs
    vmem = pl.BlockSpec(memory_space=pltpu.VMEM)
    hbm = pl.BlockSpec(memory_space=pltpu.HBM)
    dma = pltpu.SemaphoreType.DMA
    V = pltpu.VMEM
    outs = pl.pallas_call(
        functools.partial(kernel, levels, reqs, T, R, SYS, CTX, C, M, PAIR),
        out_shape=(
            jax.ShapeDtypeStruct((HEADS, T * R, D), F32),
            jax.ShapeDtypeStruct((rq, D), F32),
            jax.ShapeDtypeStruct((rq, D), F32),
            jax.ShapeDtypeStruct((C, CL, D), F32),
            jax.ShapeDtypeStruct((C, CL, D), F32),
            jax.ShapeDtypeStruct((T * R, D), F32),
            jax.ShapeDtypeStruct((T * R, D), F32),
        ),
        in_specs=[hbm] * 11,
        out_specs=(hbm,) + (vmem,) * 6,
        scratch_shapes=[
            V((T, R, HEADS * D), BF16),
            V((T, R, HEADS * D), BF16),
            V((T, R, D), BF16),
            V((T, R, D), BF16),
            pltpu.SMEM((R,), jnp.int32),
            pltpu.SMEM((R,), jnp.int32),
            pltpu.SMEM((C,), jnp.int32),
            dma((9 + 2 * C,)),
            V((HEADS, T * R, D), F32),
            dma(()),
            V((HEADS, T * R, D), F32),
            V((HEADS, T * R, D), F32),
            V((2, T * R, D), F32),
            V((R, 2, OWN, D), BF16),
            V((levels, SH, D), BF16),
            V((PAIR, 2, N, D), BF16),
            V((R, M, D), BF16),
            V((R, M, D), BF16),
            V((PAIR, N, M), F32),
            V((PAIR, N, M), F32),
            V((PAIR, N, M), BF16),
            V((PAIR, N, M), BF16),
            V((PAIR, 2, OWN, D), F32),
            V((R, 2, T, D), F32),
            V((R, levels, 2, T, D), BF16),
            V((R, levels, 2, T, D), BF16),
            V((2, SYS, D), F32),
            V((2, C, CTX, D), F32),
            V((levels, SH, D), BF16),
            V((levels, SH, D), BF16),
            V((reqs, 2 * rq, D), F32),
            V((reqs, 2 * rq, D), F32),
            dma((R, levels)), dma((R, levels)),
            dma((levels,)), dma((levels,)),
            dma((R, levels)), dma((R, levels)),
            dma((levels,)), dma((levels,)),
            dma((reqs,)), dma((reqs,)),
        ],
        compiler_params=pltpu.CompilerParams(
            collective_id=0, has_side_effects=True, vmem_limit_bytes=56 * 2**20
        ),
        cost_estimate=pl.CostEstimate(
            flops=10 * R * M * N * D, bytes_accessed=10 * T * R * HEADS * D,
            transcendentals=R * M * N,
        ),
    )(queries, out_grad, resp_key, resp_value, sys_key, sys_value, ctx_key, ctx_value,
      parent, resp_len, ctx_len)
    dq, dsk, dsv, dck, dcv, drk, drv = outs
    finals = (dq.reshape(HEADS, T, R, D), dsk, dsv, dck, dcv,
              drk.reshape(T, R, D), drv.reshape(T, R, D))
    shapes = ((T, R, HEADS * D),) + tuple(a.shape for a in finals[1:])
    return pl.pallas_call(
        write_out,
        out_shape=tuple(jax.ShapeDtypeStruct(shape, F32) for shape in shapes),
        in_specs=[hbm] * 7,
        out_specs=(hbm,) * 7,
        scratch_shapes=[V(a.shape, F32) for a in finals] + [dma((HEADS + 6,)), dma((HEADS + 6,))],
        compiler_params=pltpu.CompilerParams(vmem_limit_bytes=56 * 2**20),
    )(*finals)


def solution(mesh):
    return jax.shard_map(
        functools.partial(shards, mesh.shape["level"], mesh.shape["req"]),
        mesh=mesh,
        in_specs=(
            P("level", "req", None),
            P("level", "req", None),
            P("level", "req", None),
            P("level", "req", None),
            P("level", None),
            P("level", None),
            P("req", "level", None),
            P("req", "level", None),
            P("req"),
            P("req"),
            P("req"),
        ),
        out_specs=(
            P("level", "req", None),
            P(("level", "req"), None),
            P(("level", "req"), None),
            P("req", "level", None),
            P("req", "level", None),
            P("level", "req", None),
            P("level", "req", None),
        ),
        check_vma=False,
    )
```

```python
import functools
import math

import jax
import jax.numpy as jnp
from jax import lax
from jax.experimental import pallas as pl
from jax.experimental.pallas import tpu as pltpu
from jax.sharding import PartitionSpec as P

HEADS = 7
D = 128
NEGATIVE = -1e30
SCALING = D ** (-0.5)
SCALING2 = SCALING * math.log2(math.e)
F32 = jnp.float32
BF16 = jnp.bfloat16
MESH = pl.DeviceIdType.MESH


def nt(a, b):
    return lax.dot_general(a, b, (((1,), (1,)), ((), ())), preferred_element_type=F32)


def tn(a, b):
    return lax.dot_general(a, b, (((0,), (0,)), ((), ())), preferred_element_type=F32)


def nn(a, b):
    return jnp.dot(a, b, preferred_element_type=F32)


def kernel(
    levels, reqs, T, R, SYS, CTX, C, M, PAIR,
    q_in, g_in, rk_in, rv_in, sk_in, sv_in, ck_in, cv_in, parent_in, rlen_in, clen_in,
    dq_out, dsk_ref, dsv_ref, dck_ref, dcv_ref, drk_ref, drv_ref,
    q_ref, g_ref, rk_ref, rv_ref, parent, rlen, clen, in_s, dq_ref, dq_s, qf, gf, kvf, kv, shared, keys, q_s, g_s, s_s, p_s, ch_s, sl_s, own_part, own_grad, gsend, grecv,
    shared_acc_sys, shared_acc_ctx, csend, crecv, tsend, trecv,
    kv_ss, kv_rs, sh_ss, sh_rs, gr_ss, gr_rs, cs_ss, cs_rs, t_ss, t_rs,
):
    me = lax.axis_index("level")
    mq = lax.axis_index("req")
    SL, CL = SYS // levels, CTX // levels
    K0, V0 = 0, SL + C * CL
    OWN = levels * T

    barrier = pltpu.get_barrier_semaphore()
    for b in range(levels):
        @pl.when(b != me)
        def _(b=b):
            pl.semaphore_signal(barrier, inc=1, device_id=(b, mq), device_id_type=MESH)
    for b in range(reqs):
        @pl.when(b != mq)
        def _(b=b):
            pl.semaphore_signal(barrier, inc=1, device_id=(me, b), device_id_type=MESH)

    loads = []

    def load(src, dst):
        copy = pltpu.make_async_copy(src, dst, in_s.at[len(loads)])
        copy.start()
        loads.append(copy)

    load(rk_in, rk_ref)
    load(rv_in, rv_ref)
    load(sk_in, shared.at[me, K0:K0 + SL])
    load(sv_in, shared.at[me, V0:V0 + SL])
    for c in range(C):
        load(ck_in.at[c], shared.at[me, K0 + SL + c * CL:K0 + SL + (c + 1) * CL])
        load(cv_in.at[c], shared.at[me, V0 + SL + c * CL:V0 + SL + (c + 1) * CL])
    first = len(loads)
    load(q_in, q_ref)
    load(g_in, g_ref)
    load(parent_in, parent)
    load(rlen_in, rlen)
    load(clen_in, clen)

    mine = pl.ds(pl.multiple_of(me * T, T), T)
    for copy in loads[:2]:
        copy.wait()
    kvf[0] = rk_ref[...].astype(F32).reshape(T * R, D)
    kvf[1] = rv_ref[...].astype(F32).reshape(T * R, D)
    for r in range(R):
        for i in range(2):
            kv[r, i, mine, :] = kvf[i, pl.ds(r, T, stride=R), :].astype(BF16)
    for b in range(levels):
        @pl.when(b > me)
        def _(b=b):
            kv[:, :, b * T:(b + 1) * T, :] = jnp.zeros((R, 2, T, D), BF16)

    for copy in loads[2:first]:
        copy.wait()
    pl.semaphore_wait(barrier, levels + reqs - 2)

    def shared_copy(dst, src):
        return pltpu.make_async_remote_copy(
            src_ref=shared.at[me], dst_ref=shared.at[me],
            send_sem=sh_ss.at[dst], recv_sem=sh_rs.at[src],
            device_id=(dst, mq), device_id_type=MESH)

    def kv_copy(r, dst, src):
        return pltpu.make_async_remote_copy(
            src_ref=kv.at[r, :, mine, :], dst_ref=kv.at[r, :, mine, :],
            send_sem=kv_ss.at[r, dst], recv_sem=kv_rs.at[r, src],
            device_id=(dst, mq), device_id_type=MESH)

    def grad_copy(r, dst, src):
        return pltpu.make_async_remote_copy(
            src_ref=gsend.at[r, dst], dst_ref=grecv.at[r, src],
            send_sem=gr_ss.at[r, dst], recv_sem=gr_rs.at[r, src],
            device_id=(dst, mq), device_id_type=MESH)

    def sum_copy(dst, src):
        return pltpu.make_async_remote_copy(
            src_ref=csend.at[dst], dst_ref=crecv.at[src],
            send_sem=cs_ss.at[dst], recv_sem=cs_rs.at[src],
            device_id=(dst, mq), device_id_type=MESH)

    def total_copy(dst, src):
        return pltpu.make_async_remote_copy(
            src_ref=tsend.at[dst], dst_ref=trecv.at[src],
            send_sem=t_ss.at[dst], recv_sem=t_rs.at[src],
            device_id=(me, dst), device_id_type=MESH)

    for b in range(levels):
        @pl.when(b != me)
        def _(b=b):
            shared_copy(b, me).start()

    def send_keys(r, carry):
        for b in range(levels):
            @pl.when(b > me)
            def _(b=b):
                kv_copy(r, b, me).start()
        return carry

    lax.fori_loop(0, R, send_keys, 0)

    for copy in loads[first:]:
        copy.wait()
    for h in range(HEADS):
        qf[h] = q_ref[:, :, h * D:(h + 1) * D].astype(F32).reshape(T * R, D)
        gf[h] = g_ref[:, :, h * D:(h + 1) * D].astype(F32).reshape(T * R, D)
    row_at = me * T + lax.broadcasted_iota(jnp.int32, (T, D), 0)

    def arrange(r, carry):
        live = row_at < rlen[r]
        rows = pl.ds(r, T, stride=R)
        for h in range(HEADS):
            q_s[r, h * T:(h + 1) * T, :] = qf[h, rows, :].astype(BF16)
            g_s[r, h * T:(h + 1) * T, :] = jnp.where(live, gf[h, rows, :], 0.0).astype(BF16)
        if M > HEADS * T:
            q_s[r, HEADS * T:, :] = jnp.zeros((M - HEADS * T, D), BF16)
            g_s[r, HEADS * T:, :] = jnp.zeros((M - HEADS * T, D), BF16)
        return carry

    lax.fori_loop(0, R, arrange, 0)
    shared_acc_sys[...] = jnp.zeros(shared_acc_sys.shape, F32)
    shared_acc_ctx[...] = jnp.zeros(shared_acc_ctx.shape, F32)
    crecv[me] = jnp.zeros(crecv.shape[1:], BF16)

    for b in range(levels):
        @pl.when(b != me)
        def _(b=b):
            shared_copy(b, b).wait_recv()

    chunks = []
    for kind, begin, length in (("sys", 0, SYS), ("ctx", SYS, CTX), ("own", SYS + CTX, OWN)):
        width = min(32, length)
        for start in range(0, length, width):
            chunks.append((kind, start, width, slice(begin + start, begin + start + width)))
    row_of_lane = me * T + lax.rem(lax.broadcasted_iota(jnp.int32, (1, M), 1), T)
    for j in range(PAIR):
        for i, base in ((0, K0), (1, V0)):
            keys[j, i, :SYS, :] = shared[:, base:base + SL, :].reshape(SYS, D)

    def prepare(j, r):
        where_ctx = parent[r] - mq * C
        limit = jnp.int32(0)
        chosen = []
        for c in range(C):
            chosen.append(jnp.where(where_ctx == c, 1.0, 0.0))
            limit = limit + jnp.where(where_ctx == c, clen[c], 0)
        for i, base in ((0, K0), (1, V0)):
            picked = jnp.zeros((levels, CL, D), F32)
            for c in range(C):
                at = base + SL + c * CL
                picked = picked + chosen[c] * shared[:, at:at + CL, :].astype(F32)
            keys[j, i, SYS:SYS + CTX, :] = picked.astype(BF16).reshape(CTX, D)
            keys[j, i, SYS + CTX:, :] = kv[r, i]
        s_s[j] = nt(keys[j, 0], q_s[r])
        p_s[j] = nt(keys[j, 1], g_s[r])
        return chosen, limit

    def maxima(j, limit):
        tops = jnp.full((8, M), NEGATIVE, F32)
        for kind, start, width, at in chunks:
            scores = s_s[j, at, :] * SCALING2
            places = lax.broadcasted_iota(jnp.int32, (width, M), 0)
            if kind == "ctx":
                scores = jnp.where(places < limit - start, scores, NEGATIVE)
            if kind == "own":
                scores = jnp.where(places <= row_of_lane - start, scores, NEGATIVE)
            if kind != "sys":
                s_s[j, at, :] = scores
            tops = jnp.maximum(tops, jnp.max(scores.reshape(width // 8, 8, M), axis=0))
        return jnp.max(tops, axis=0, keepdims=True)

    def sums(j, top):
        totals = jnp.zeros((8, M), F32)
        running = jnp.zeros((8, M), F32)
        for kind, start, width, at in chunks:
            scores = s_s[j, at, :]
            if kind == "sys":
                scores = scores * SCALING2
            weights = jnp.exp2(scores - top)
            s_s[j, at, :] = weights
            totals = totals + jnp.sum(weights.reshape(width // 8, 8, M), axis=0)
            parts = weights * p_s[j, at, :]
            running = running + jnp.sum(parts.reshape(width // 8, 8, M), axis=0)
        inverse = 1.0 / jnp.sum(totals, axis=0, keepdims=True)
        return inverse, jnp.sum(running, axis=0, keepdims=True) * inverse

    def roundings(j, inverse, deltas):
        for kind, start, width, at in chunks:
            chances = s_s[j, at, :] * inverse
            ch_s[j, at, :] = chances.astype(BF16)
            sl_s[j, at, :] = (chances * (p_s[j, at, :] - deltas)).astype(BF16)

    def gradients(j, r, chosen):
        dk = nn(sl_s[j], q_s[r]) * SCALING
        dv = nn(ch_s[j], g_s[r])
        for i, grad in ((0, dk), (1, dv)):
            shared_acc_sys[i] += grad[:SYS]
            for c in range(C):
                shared_acc_ctx[i, c] += grad[SYS:SYS + CTX] * chosen[c]
            own_part[j, i] = grad[SYS + CTX:]
        dq_rows = jnp.transpose(tn(keys[j, 0], sl_s[j])) * SCALING
        for h in range(HEADS):
            dq_ref[h, pl.ds(r, T, stride=R), :] = dq_rows[h * T:(h + 1) * T]

    def responses(step, carry):
        rs = [step * PAIR + j for j in range(PAIR)]
        for b in range(levels):
            @pl.when(b < me)
            def _(b=b):
                for r in rs:
                    kv_copy(r, b, b).wait_recv()
        ready = [prepare(j, r) for j, r in enumerate(rs)]
        tops = [maxima(j, ready[j][1]) for j in range(PAIR)]
        for j, r in enumerate(rs):
            roundings(j, *sums(j, tops[j]))
        for j, r in enumerate(rs):
            gradients(j, r, ready[j][0])
        for j, r in enumerate(rs):
            own_grad[r] = own_part[j, :, mine, :]
        for b in range(levels):
            @pl.when(b < me)
            def _(b=b):
                for j, r in enumerate(rs):
                    gsend[r, b] = own_part[j, :, b * T:(b + 1) * T, :].astype(BF16)
                    grad_copy(r, b, me).start()
        return carry

    lax.fori_loop(0, R // PAIR, responses, 0)
    dq_copy = pltpu.make_async_copy(dq_ref, dq_out, dq_s)
    dq_copy.start()

    for b in range(levels):
        @pl.when(b != me)
        def _(b=b):
            for which, base in ((0, K0), (1, V0)):
                csend[b, base:base + SL] = shared_acc_sys[which, b * SL:(b + 1) * SL].astype(BF16)
                for c in range(C):
                    at = base + SL + c * CL
                    csend[b, at:at + CL] = shared_acc_ctx[which, c, b * CL:(b + 1) * CL].astype(BF16)
            sum_copy(b, me).start()

    def finish(r, carry):
        for b in range(levels):
            @pl.when(b > me)
            def _(b=b):
                grad_copy(r, b, b).wait_recv()
                own_grad[r] += grecv[r, b].astype(F32)
        rows = pl.ds(r, T, stride=R)
        drk_ref[rows, :] = own_grad[r, 0]
        drv_ref[rows, :] = own_grad[r, 1]
        return carry

    lax.fori_loop(0, R - 1, finish, 0)

    for b in range(levels):
        @pl.when(b != me)
        def _(b=b):
            sum_copy(b, b).wait_recv()
    rq = SL // reqs
    sys_rows = pl.ds(pl.multiple_of(me * SL, SL), SL)
    ctx_rows = pl.ds(pl.multiple_of(me * CL, CL), CL)
    for which, base in ((0, K0), (1, V0)):
        total = shared_acc_sys[which, sys_rows, :]
        for b in range(levels):
            total = total + crecv[b, base:base + SL, :].astype(F32)
        for b in range(reqs):
            tsend[b, which * rq:(which + 1) * rq, :] = total[b * rq:(b + 1) * rq]
    for b in range(reqs):
        @pl.when(b != mq)
        def _(b=b):
            total_copy(b, mq).start()
    trecv[mq] = tsend[mq]
    for which, base, out in ((0, K0, dck_ref), (1, V0, dcv_ref)):
        for c in range(C):
            at = base + SL + c * CL
            total = shared_acc_ctx[which, c, ctx_rows, :]
            for b in range(levels):
                total = total + crecv[b, at:at + CL, :].astype(F32)
            out[c] = total
    finish(R - 1, 0)

    for b in range(levels):
        @pl.when(b != me)
        def _(b=b):
            shared_copy(b, me).wait_send()
            sum_copy(b, me).wait_send()

    def sent(r, carry):
        for b in range(levels):
            @pl.when(b > me)
            def _(b=b):
                kv_copy(r, b, me).wait_send()

            @pl.when(b < me)
            def _(b=b):
                grad_copy(r, b, me).wait_send()
        return carry

    lax.fori_loop(0, R, sent, 0)
    for b in range(reqs):
        @pl.when(b != mq)
        def _(b=b):
            total_copy(b, mq).wait_send()
            total_copy(b, b).wait_recv()
    dq_copy.wait()
    grand = trecv[0]
    for b in range(1, reqs):
        grand = grand + trecv[b]
    dsk_ref[...] = grand[:rq]
    dsv_ref[...] = grand[rq:]


def write_out(*refs):
    ins, outs, held, sem_in, sem_out = refs[:7], refs[7:14], refs[14:21], refs[21], refs[22]
    pieces = [(ins[0].at[h], held[0].at[h], outs[0].at[:, :, h * D:(h + 1) * D])
              for h in range(HEADS)]
    pieces += list(zip(ins[1:], held[1:], outs[1:]))
    reads = [pltpu.make_async_copy(src, mid, sem_in.at[i])
             for i, (src, mid, _) in enumerate(pieces)]
    writes = [pltpu.make_async_copy(mid, dst, sem_out.at[i])
              for i, (_, mid, dst) in enumerate(pieces)]
    for copy in reads:
        copy.start()
    for read, write in zip(reads, writes):
        read.wait()
        write.start()
    for copy in writes:
        copy.wait()


def shards(levels, reqs, queries, out_grad, resp_key, resp_value, sys_key, sys_value,
           ctx_key, ctx_value, parent, resp_len, ctx_len):
    T, R, _ = queries.shape
    SL, CL, C = sys_key.shape[0], ctx_key.shape[1], ctx_key.shape[0]
    SYS, CTX = SL * levels, CL * levels
    M = -(-HEADS * T // 128) * 128
    OWN = levels * T
    PAIR = 2 if R % 2 == 0 else 1
    N = SYS + CTX + OWN
    SH = 2 * (SL + C * CL)
    rq = SL // reqs
    vmem = pl.BlockSpec(memory_space=pltpu.VMEM)
    hbm = pl.BlockSpec(memory_space=pltpu.HBM)
    dma = pltpu.SemaphoreType.DMA
    V = pltpu.VMEM
    outs = pl.pallas_call(
        functools.partial(kernel, levels, reqs, T, R, SYS, CTX, C, M, PAIR),
        out_shape=(
            jax.ShapeDtypeStruct((HEADS, T * R, D), F32),
            jax.ShapeDtypeStruct((rq, D), F32),
            jax.ShapeDtypeStruct((rq, D), F32),
            jax.ShapeDtypeStruct((C, CL, D), F32),
            jax.ShapeDtypeStruct((C, CL, D), F32),
            jax.ShapeDtypeStruct((T * R, D), F32),
            jax.ShapeDtypeStruct((T * R, D), F32),
        ),
        in_specs=[hbm] * 11,
        out_specs=(hbm,) + (vmem,) * 6,
        scratch_shapes=[
            V((T, R, HEADS * D), BF16),
            V((T, R, HEADS * D), BF16),
            V((T, R, D), BF16),
            V((T, R, D), BF16),
            pltpu.SMEM((R,), jnp.int32),
            pltpu.SMEM((R,), jnp.int32),
            pltpu.SMEM((C,), jnp.int32),
            dma((9 + 2 * C,)),
            V((HEADS, T * R, D), F32),
            dma(()),
            V((HEADS, T * R, D), F32),
            V((HEADS, T * R, D), F32),
            V((2, T * R, D), F32),
            V((R, 2, OWN, D), BF16),
            V((levels, SH, D), BF16),
            V((PAIR, 2, N, D), BF16),
            V((R, M, D), BF16),
            V((R, M, D), BF16),
            V((PAIR, N, M), F32),
            V((PAIR, N, M), F32),
            V((PAIR, N, M), BF16),
            V((PAIR, N, M), BF16),
            V((PAIR, 2, OWN, D), F32),
            V((R, 2, T, D), F32),
            V((R, levels, 2, T, D), BF16),
            V((R, levels, 2, T, D), BF16),
            V((2, SYS, D), F32),
            V((2, C, CTX, D), F32),
            V((levels, SH, D), BF16),
            V((levels, SH, D), BF16),
            V((reqs, 2 * rq, D), F32),
            V((reqs, 2 * rq, D), F32),
            dma((R, levels)), dma((R, levels)),
            dma((levels,)), dma((levels,)),
            dma((R, levels)), dma((R, levels)),
            dma((levels,)), dma((levels,)),
            dma((reqs,)), dma((reqs,)),
        ],
        compiler_params=pltpu.CompilerParams(
            collective_id=0, has_side_effects=True, vmem_limit_bytes=56 * 2**20
        ),
        cost_estimate=pl.CostEstimate(
            flops=10 * R * M * N * D, bytes_accessed=10 * T * R * HEADS * D,
            transcendentals=R * M * N,
        ),
    )(queries, out_grad, resp_key, resp_value, sys_key, sys_value, ctx_key, ctx_value,
      parent, resp_len, ctx_len)
    dq, dsk, dsv, dck, dcv, drk, drv = outs
    finals = (dq.reshape(HEADS, T, R, D), dsk, dsv, dck, dcv,
              drk.reshape(T, R, D), drv.reshape(T, R, D))
    shapes = ((T, R, HEADS * D),) + tuple(a.shape for a in finals[1:])
    return pl.pallas_call(
        write_out,
        out_shape=tuple(jax.ShapeDtypeStruct(shape, F32) for shape in shapes),
        in_specs=[hbm] * 7,
        out_specs=(hbm,) * 7,
        scratch_shapes=[V(a.shape, F32) for a in finals] + [dma((HEADS + 6,)), dma((HEADS + 6,))],
        compiler_params=pltpu.CompilerParams(vmem_limit_bytes=56 * 2**20),
    )(*finals)


def solution(mesh):
    return jax.shard_map(
        functools.partial(shards, mesh.shape["level"], mesh.shape["req"]),
        mesh=mesh,
        in_specs=(
            P("level", "req", None),
            P("level", "req", None),
            P("level", "req", None),
            P("level", "req", None),
            P("level", None),
            P("level", None),
            P("req", "level", None),
            P("req", "level", None),
            P("req"),
            P("req"),
            P("req"),
        ),
        out_specs=(
            P("level", "req", None),
            P(("level", "req"), None),
            P(("level", "req"), None),
            P("req", "level", None),
            P("req", "level", None),
            P("level", "req", None),
            P("level", "req", None),
        ),
        check_vma=False,
    )
```

```python
import functools
import math

import jax
import jax.numpy as jnp
from jax import lax
from jax.experimental import pallas as pl
from jax.experimental.pallas import tpu as pltpu
from jax.sharding import PartitionSpec as P

HEADS = 7
D = 128
NEGATIVE = -1e30
SCALING = D ** (-0.5)
SCALING2 = SCALING * math.log2(math.e)
F32 = jnp.float32
BF16 = jnp.bfloat16
MESH = pl.DeviceIdType.MESH


def nt(a, b):
    return lax.dot_general(a, b, (((1,), (1,)), ((), ())), preferred_element_type=F32)


def tn(a, b):
    return lax.dot_general(a, b, (((0,), (0,)), ((), ())), preferred_element_type=F32)


def nn(a, b):
    return jnp.dot(a, b, preferred_element_type=F32)


def kernel(
    levels, reqs, T, R, SYS, CTX, C, M, PAIR,
    q_in, g_in, rk_in, rv_in, sk_in, sv_in, ck_in, cv_in, parent_in, rlen_in, clen_in,
    dq_out, dsk_ref, dsv_ref, dck_ref, dcv_ref, drk_ref, drv_ref,
    q_ref, g_ref, rk_ref, rv_ref, parent, rlen, clen, in_s, dq_ref, dq_s, qf, gf, kvf, kv, shared, keys, q_s, g_s, s_s, p_s, ch_s, sl_s, own_part, own_grad, gsend, grecv,
    shared_acc_sys, shared_acc_ctx, csend, crecv, tsend, trecv,
    kv_ss, kv_rs, sh_ss, sh_rs, gr_ss, gr_rs, cs_ss, cs_rs, t_ss, t_rs,
):
    me = lax.axis_index("level")
    mq = lax.axis_index("req")
    SL, CL = SYS // levels, CTX // levels
    K0, V0 = 0, SL + C * CL
    OWN = levels * T

    barrier = pltpu.get_barrier_semaphore()
    for b in range(levels):
        @pl.when(b != me)
        def _(b=b):
            pl.semaphore_signal(barrier, inc=1, device_id=(b, mq), device_id_type=MESH)
    for b in range(reqs):
        @pl.when(b != mq)
        def _(b=b):
            pl.semaphore_signal(barrier, inc=1, device_id=(me, b), device_id_type=MESH)

    loads = []

    def load(src, dst):
        copy = pltpu.make_async_copy(src, dst, in_s.at[len(loads)])
        copy.start()
        loads.append(copy)

    load(rk_in, rk_ref)
    load(rv_in, rv_ref)
    load(sk_in, shared.at[me, K0:K0 + SL])
    load(sv_in, shared.at[me, V0:V0 + SL])
    for c in range(C):
        load(ck_in.at[c], shared.at[me, K0 + SL + c * CL:K0 + SL + (c + 1) * CL])
        load(cv_in.at[c], shared.at[me, V0 + SL + c * CL:V0 + SL + (c + 1) * CL])
    first = len(loads)
    load(q_in, q_ref)
    load(g_in, g_ref)
    load(parent_in, parent)
    load(rlen_in, rlen)
    load(clen_in, clen)

    mine = pl.ds(pl.multiple_of(me * T, T), T)
    for copy in loads[:2]:
        copy.wait()
    kvf[0] = rk_ref[...].astype(F32).reshape(T * R, D)
    kvf[1] = rv_ref[...].astype(F32).reshape(T * R, D)
    for r in range(R):
        for i in range(2):
            kv[r, i, mine, :] = kvf[i, pl.ds(r, T, stride=R), :].astype(BF16)
    for b in range(levels):
        @pl.when(b > me)
        def _(b=b):
            kv[:, :, b * T:(b + 1) * T, :] = jnp.zeros((R, 2, T, D), BF16)

    for copy in loads[2:first]:
        copy.wait()
    pl.semaphore_wait(barrier, levels + reqs - 2)

    def shared_copy(dst, src):
        return pltpu.make_async_remote_copy(
            src_ref=shared.at[me], dst_ref=shared.at[me],
            send_sem=sh_ss.at[dst], recv_sem=sh_rs.at[src],
            device_id=(dst, mq), device_id_type=MESH)

    def kv_copy(r, dst, src):
        return pltpu.make_async_remote_copy(
            src_ref=kv.at[r, :, mine, :], dst_ref=kv.at[r, :, mine, :],
            send_sem=kv_ss.at[r, dst], recv_sem=kv_rs.at[r, src],
            device_id=(dst, mq), device_id_type=MESH)

    def grad_copy(r, dst, src):
        return pltpu.make_async_remote_copy(
            src_ref=gsend.at[r, dst], dst_ref=grecv.at[r, src],
            send_sem=gr_ss.at[r, dst], recv_sem=gr_rs.at[r, src],
            device_id=(dst, mq), device_id_type=MESH)

    def sum_copy(dst, src):
        return pltpu.make_async_remote_copy(
            src_ref=csend.at[dst], dst_ref=crecv.at[src],
            send_sem=cs_ss.at[dst], recv_sem=cs_rs.at[src],
            device_id=(dst, mq), device_id_type=MESH)

    def total_copy(dst, src):
        return pltpu.make_async_remote_copy(
            src_ref=tsend.at[dst], dst_ref=trecv.at[src],
            send_sem=t_ss.at[dst], recv_sem=t_rs.at[src],
            device_id=(me, dst), device_id_type=MESH)

    for b in range(levels):
        @pl.when(b != me)
        def _(b=b):
            shared_copy(b, me).start()

    def send_keys(r, carry):
        for b in range(levels):
            @pl.when(b > me)
            def _(b=b):
                kv_copy(r, b, me).start()
        return carry

    lax.fori_loop(0, R, send_keys, 0)

    for copy in loads[first:]:
        copy.wait()
    for h in range(HEADS):
        qf[h] = q_ref[:, :, h * D:(h + 1) * D].astype(F32).reshape(T * R, D)
        gf[h] = g_ref[:, :, h * D:(h + 1) * D].astype(F32).reshape(T * R, D)
    row_at = me * T + lax.broadcasted_iota(jnp.int32, (T, D), 0)

    def arrange(r, carry):
        live = row_at < rlen[r]
        rows = pl.ds(r, T, stride=R)
        for h in range(HEADS):
            q_s[r, h * T:(h + 1) * T, :] = qf[h, rows, :].astype(BF16)
            g_s[r, h * T:(h + 1) * T, :] = jnp.where(live, gf[h, rows, :], 0.0).astype(BF16)
        if M > HEADS * T:
            q_s[r, HEADS * T:, :] = jnp.zeros((M - HEADS * T, D), BF16)
            g_s[r, HEADS * T:, :] = jnp.zeros((M - HEADS * T, D), BF16)
        return carry

    lax.fori_loop(0, R, arrange, 0)
    shared_acc_sys[...] = jnp.zeros(shared_acc_sys.shape, F32)
    shared_acc_ctx[...] = jnp.zeros(shared_acc_ctx.shape, F32)
    crecv[me] = jnp.zeros(crecv.shape[1:], BF16)

    for b in range(levels):
        @pl.when(b != me)
        def _(b=b):
            shared_copy(b, b).wait_recv()

    chunks = []
    for kind, begin, length in (("sys", 0, SYS), ("ctx", SYS, CTX), ("own", SYS + CTX, OWN)):
        width = min(32, length)
        for start in range(0, length, width):
            chunks.append((kind, start, width, slice(begin + start, begin + start + width)))
    row_of_lane = me * T + lax.rem(lax.broadcasted_iota(jnp.int32, (1, M), 1), T)
    for j in range(PAIR):
        for i, base in ((0, K0), (1, V0)):
            keys[j, i, :SYS, :] = shared[:, base:base + SL, :].reshape(SYS, D)

    def prepare(j, r):
        where_ctx = parent[r] - mq * C
        limit = jnp.int32(0)
        chosen = []
        for c in range(C):
            chosen.append(jnp.where(where_ctx == c, 1.0, 0.0))
            limit = limit + jnp.where(where_ctx == c, clen[c], 0)
        for i, base in ((0, K0), (1, V0)):
            picked = jnp.zeros((levels, CL, D), F32)
            for c in range(C):
                at = base + SL + c * CL
                picked = picked + chosen[c] * shared[:, at:at + CL, :].astype(F32)
            keys[j, i, SYS:SYS + CTX, :] = picked.astype(BF16).reshape(CTX, D)
            keys[j, i, SYS + CTX:, :] = kv[r, i]
        s_s[j] = nt(keys[j, 0], q_s[r])
        p_s[j] = nt(keys[j, 1], g_s[r])
        return chosen, limit

    def maxima(j, limit):
        tops = jnp.full((8, M), NEGATIVE, F32)
        for kind, start, width, at in chunks:
            scores = s_s[j, at, :] * SCALING2
            places = lax.broadcasted_iota(jnp.int32, (width, M), 0)
            if kind == "ctx":
                scores = jnp.where(places < limit - start, scores, NEGATIVE)
            if kind == "own":
                scores = jnp.where(places <= row_of_lane - start, scores, NEGATIVE)
            if kind != "sys":
                s_s[j, at, :] = scores
            tops = jnp.maximum(tops, jnp.max(scores.reshape(width // 8, 8, M), axis=0))
        return jnp.max(tops, axis=0, keepdims=True)

    def sums(j, top):
        totals = jnp.zeros((8, M), F32)
        running = jnp.zeros((8, M), F32)
        for kind, start, width, at in chunks:
            scores = s_s[j, at, :]
            if kind == "sys":
                scores = scores * SCALING2
            weights = jnp.exp2(scores - top)
            s_s[j, at, :] = weights
            totals = totals + jnp.sum(weights.reshape(width // 8, 8, M), axis=0)
            parts = weights * p_s[j, at, :]
            running = running + jnp.sum(parts.reshape(width // 8, 8, M), axis=0)
        inverse = 1.0 / jnp.sum(totals, axis=0, keepdims=True)
        return inverse, jnp.sum(running, axis=0, keepdims=True) * inverse

    def roundings(j, inverse, deltas):
        for kind, start, width, at in chunks:
            chances = s_s[j, at, :] * inverse
            ch_s[j, at, :] = chances.astype(BF16)
            sl_s[j, at, :] = (chances * (p_s[j, at, :] - deltas)).astype(BF16)

    def send_sums():
        for b in range(levels):
            @pl.when(b != me)
            def _(b=b):
                for i, base in ((0, K0), (1, V0)):
                    rows = shared_acc_sys[i, b * SL:(b + 1) * SL]
                    csend[b, base:base + SL] = rows.astype(BF16)
                    for c in range(C):
                        at = base + SL + c * CL
                        rows = shared_acc_ctx[i, c, b * CL:(b + 1) * CL]
                        csend[b, at:at + CL] = rows.astype(BF16)
                sum_copy(b, me).start()

    def one_response(r, last):
        for b in range(levels):
            @pl.when(b < me)
            def _(b=b):
                kv_copy(r, b, b).wait_recv()
        chosen, limit = prepare(0, r)
        roundings(0, *sums(0, maxima(0, limit)))
        for i, grad in ((0, nn(sl_s[0], q_s[r]) * SCALING), (1, nn(ch_s[0], g_s[r]))):
            shared_acc_sys[i] += grad[:SYS]
            for c in range(C):
                shared_acc_ctx[i, c] += grad[SYS:SYS + CTX] * chosen[c]
            own_part[0, i] = grad[SYS + CTX:]
        if last:
            send_sums()
        for b in range(levels):
            @pl.when(b < me)
            def _(b=b):
                gsend[r, b] = own_part[0, :, b * T:(b + 1) * T, :].astype(BF16)
                grad_copy(r, b, me).start()
        own_grad[r] = own_part[0, :, mine, :]
        dq_rows = jnp.transpose(tn(keys[0, 0], sl_s[0])) * SCALING
        for h in range(HEADS):
            dq_ref[h, pl.ds(r, T, stride=R), :] = dq_rows[h * T:(h + 1) * T]

    def step(r, carry):
        one_response(r, False)
        return carry

    lax.fori_loop(0, R - 1, step, 0)
    one_response(R - 1, True)
    dq_copy = pltpu.make_async_copy(dq_ref, dq_out, dq_s)
    dq_copy.start()

    def finish(r, carry):
        for b in range(levels):
            @pl.when(b > me)
            def _(b=b):
                grad_copy(r, b, b).wait_recv()
                own_grad[r] += grecv[r, b].astype(F32)
        rows = pl.ds(r, T, stride=R)
        drk_ref[rows, :] = own_grad[r, 0]
        drv_ref[rows, :] = own_grad[r, 1]
        return carry

    lax.fori_loop(0, R - 1, finish, 0)

    for b in range(levels):
        @pl.when(b != me)
        def _(b=b):
            sum_copy(b, b).wait_recv()
    rq = SL // reqs
    sys_rows = pl.ds(pl.multiple_of(me * SL, SL), SL)
    ctx_rows = pl.ds(pl.multiple_of(me * CL, CL), CL)
    for which, base in ((0, K0), (1, V0)):
        total = shared_acc_sys[which, sys_rows, :]
        for b in range(levels):
            total = total + crecv[b, base:base + SL, :].astype(F32)
        for b in range(reqs):
            tsend[b, which * rq:(which + 1) * rq, :] = total[b * rq:(b + 1) * rq]
    for b in range(reqs):
        @pl.when(b != mq)
        def _(b=b):
            total_copy(b, mq).start()
    trecv[mq] = tsend[mq]
    for which, base, out in ((0, K0, dck_ref), (1, V0, dcv_ref)):
        for c in range(C):
            at = base + SL + c * CL
            total = shared_acc_ctx[which, c, ctx_rows, :]
            for b in range(levels):
                total = total + crecv[b, at:at + CL, :].astype(F32)
            out[c] = total
    finish(R - 1, 0)

    for b in range(levels):
        @pl.when(b != me)
        def _(b=b):
            shared_copy(b, me).wait_send()
            sum_copy(b, me).wait_send()

    def sent(r, carry):
        for b in range(levels):
            @pl.when(b > me)
            def _(b=b):
                kv_copy(r, b, me).wait_send()

            @pl.when(b < me)
            def _(b=b):
                grad_copy(r, b, me).wait_send()
        return carry

    lax.fori_loop(0, R, sent, 0)
    for b in range(reqs):
        @pl.when(b != mq)
        def _(b=b):
            total_copy(b, mq).wait_send()
            total_copy(b, b).wait_recv()
    dq_copy.wait()
    grand = trecv[0]
    for b in range(1, reqs):
        grand = grand + trecv[b]
    dsk_ref[...] = grand[:rq]
    dsv_ref[...] = grand[rq:]


def write_out(*refs):
    ins, outs, held, sem_in, sem_out = refs[:7], refs[7:14], refs[14:21], refs[21], refs[22]
    pieces = [(ins[0].at[h], held[0].at[h], outs[0].at[:, :, h * D:(h + 1) * D])
              for h in range(HEADS)]
    pieces += list(zip(ins[1:], held[1:], outs[1:]))
    reads = [pltpu.make_async_copy(src, mid, sem_in.at[i])
             for i, (src, mid, _) in enumerate(pieces)]
    writes = [pltpu.make_async_copy(mid, dst, sem_out.at[i])
              for i, (_, mid, dst) in enumerate(pieces)]
    for copy in reads:
        copy.start()
    for read, write in zip(reads, writes):
        read.wait()
        write.start()
    for copy in writes:
        copy.wait()


def shards(levels, reqs, queries, out_grad, resp_key, resp_value, sys_key, sys_value,
           ctx_key, ctx_value, parent, resp_len, ctx_len):
    T, R, _ = queries.shape
    SL, CL, C = sys_key.shape[0], ctx_key.shape[1], ctx_key.shape[0]
    SYS, CTX = SL * levels, CL * levels
    M = -(-HEADS * T // 128) * 128
    OWN = levels * T
    PAIR = 1
    N = SYS + CTX + OWN
    SH = 2 * (SL + C * CL)
    rq = SL // reqs
    vmem = pl.BlockSpec(memory_space=pltpu.VMEM)
    hbm = pl.BlockSpec(memory_space=pltpu.HBM)
    dma = pltpu.SemaphoreType.DMA
    V = pltpu.VMEM
    outs = pl.pallas_call(
        functools.partial(kernel, levels, reqs, T, R, SYS, CTX, C, M, PAIR),
        out_shape=(
            jax.ShapeDtypeStruct((HEADS, T * R, D), F32),
            jax.ShapeDtypeStruct((rq, D), F32),
            jax.ShapeDtypeStruct((rq, D), F32),
            jax.ShapeDtypeStruct((C, CL, D), F32),
            jax.ShapeDtypeStruct((C, CL, D), F32),
            jax.ShapeDtypeStruct((T * R, D), F32),
            jax.ShapeDtypeStruct((T * R, D), F32),
        ),
        in_specs=[hbm] * 11,
        out_specs=(hbm,) + (vmem,) * 6,
        scratch_shapes=[
            V((T, R, HEADS * D), BF16),
            V((T, R, HEADS * D), BF16),
            V((T, R, D), BF16),
            V((T, R, D), BF16),
            pltpu.SMEM((R,), jnp.int32),
            pltpu.SMEM((R,), jnp.int32),
            pltpu.SMEM((C,), jnp.int32),
            dma((9 + 2 * C,)),
            V((HEADS, T * R, D), F32),
            dma(()),
            V((HEADS, T * R, D), F32),
            V((HEADS, T * R, D), F32),
            V((2, T * R, D), F32),
            V((R, 2, OWN, D), BF16),
            V((levels, SH, D), BF16),
            V((PAIR, 2, N, D), BF16),
            V((R, M, D), BF16),
            V((R, M, D), BF16),
            V((PAIR, N, M), F32),
            V((PAIR, N, M), F32),
            V((PAIR, N, M), BF16),
            V((PAIR, N, M), BF16),
            V((PAIR, 2, OWN, D), F32),
            V((R, 2, T, D), F32),
            V((R, levels, 2, T, D), BF16),
            V((R, levels, 2, T, D), BF16),
            V((2, SYS, D), F32),
            V((2, C, CTX, D), F32),
            V((levels, SH, D), BF16),
            V((levels, SH, D), BF16),
            V((reqs, 2 * rq, D), F32),
            V((reqs, 2 * rq, D), F32),
            dma((R, levels)), dma((R, levels)),
            dma((levels,)), dma((levels,)),
            dma((R, levels)), dma((R, levels)),
            dma((levels,)), dma((levels,)),
            dma((reqs,)), dma((reqs,)),
        ],
        compiler_params=pltpu.CompilerParams(
            collective_id=0, has_side_effects=True, vmem_limit_bytes=56 * 2**20
        ),
        cost_estimate=pl.CostEstimate(
            flops=10 * R * M * N * D, bytes_accessed=10 * T * R * HEADS * D,
            transcendentals=R * M * N,
        ),
    )(queries, out_grad, resp_key, resp_value, sys_key, sys_value, ctx_key, ctx_value,
      parent, resp_len, ctx_len)
    dq, dsk, dsv, dck, dcv, drk, drv = outs
    finals = (dq.reshape(HEADS, T, R, D), dsk, dsv, dck, dcv,
              drk.reshape(T, R, D), drv.reshape(T, R, D))
    shapes = ((T, R, HEADS * D),) + tuple(a.shape for a in finals[1:])
    return pl.pallas_call(
        write_out,
        out_shape=tuple(jax.ShapeDtypeStruct(shape, F32) for shape in shapes),
        in_specs=[hbm] * 7,
        out_specs=(hbm,) * 7,
        scratch_shapes=[V(a.shape, F32) for a in finals] + [dma((HEADS + 6,)), dma((HEADS + 6,))],
        compiler_params=pltpu.CompilerParams(vmem_limit_bytes=56 * 2**20),
    )(*finals)


def solution(mesh):
    return jax.shard_map(
        functools.partial(shards, mesh.shape["level"], mesh.shape["req"]),
        mesh=mesh,
        in_specs=(
            P("level", "req", None),
            P("level", "req", None),
            P("level", "req", None),
            P("level", "req", None),
            P("level", None),
            P("level", None),
            P("req", "level", None),
            P("req", "level", None),
            P("req"),
            P("req"),
            P("req"),
        ),
        out_specs=(
            P("level", "req", None),
            P(("level", "req"), None),
            P(("level", "req"), None),
            P("req", "level", None),
            P("req", "level", None),
            P("level", "req", None),
            P("level", "req", None),
        ),
        check_vma=False,
    )
```
